256 devices in a mesh: dp: 16 (over z, y_lo), ctx: 16 (over x, y_hi, core).
Axes of the slice: x: 4, y: 4 (y_hi: 2, y_lo: 2; y = y_hi * 2 + y_lo), z: 8, core: 2. Of those that a mesh axis runs over, the one named last changes fastest.
Arguments:
- queries: bfloat16 [65536, 2048], P(('dp', 'ctx')), parts along dimension 0, may hold values from -100 to 100
- keys: bfloat16 [65536, 2048], P(('dp', 'ctx')), parts along dimension 0, may hold values from -5 to 5
- values: bfloat16 [65536, 2048], P(('dp', 'ctx')), parts along dimension 0, may hold values from -6 to 6
- outputs: bfloat16 [65536, 2048], P(('dp', 'ctx')), parts along dimension 0, may hold values from -6 to 6
- out_grad: bfloat16 [65536, 2048], P(('dp', 'ctx')), parts along dimension 0, may hold values from -6 to 6
- segment_ids: int32 [65536], P(('dp', 'ctx')), parts along dimension 0, may hold values from 0 to 7, never falling along the last dimension, each value on 1 to 1536 neighbouring positions
Outputs:
- query_grad: bfloat16 [65536, 2048], P(('dp', 'ctx')), parts along dimension 0
- key_grad: bfloat16 [65536, 2048], P(('dp', 'ctx')), parts along dimension 0
- value_grad: bfloat16 [65536, 2048], P(('dp', 'ctx')), parts along dimension 0
The draws below stay inside these ranges and needn't reach their ends.
There are 16 independent parts, one for each index of `dp`. The reference program is written for one: setup_inputs(seed, part) draws one part's arguments, and reference() takes and returns one part's arrays. A program takes and returns all parts, laid end to end along the dimension named above; each array names one. Nothing has to cross between parts.
Inputs may be any that keep to these rules, and one draw needn't show every extreme that they name: `segment_ids`: ids never fall; each document holds 1 to 1536 positions, one exactly that many.
All inputs are finite; a program needn't handle non-finite values.
Results may differ from the reference program's by a relative error of at most 0.0049.
Values may be sent and summed in bfloat16 or wider, within the bound.
A program may use at most 128 MiB of HBM per device.

```python
import math
import jax
import jax.numpy as jnp
import numpy as np
from jax import lax

HEADS = 16
HEAD = 128
WINDOW = 768
SEQ = 4096
DOCS = 8
LONGEST = 1536


def base_keys(key):
    shared = jax.random.normal(jax.random.fold_in(key, 17), (SEQ, HEADS * HEAD), jnp.float32)
    shared = jnp.clip(shared, -5.0, 5.0)
    first = shared[5]
    stretched = jnp.where(first > 0, first * (5.0 / jnp.max(first)), first * (5.0 / -jnp.min(first)))
    return shared.at[5].set(jnp.clip(stretched, -5.0, 5.0))


def draw_keys(key, part):
    shared = base_keys(key)
    return shared.astype(jnp.bfloat16)


def draw_queries(key, part):
    key = jax.random.fold_in(key, 2)
    fresh = jnp.clip(jax.random.normal(key, (SEQ, HEADS * HEAD), jnp.float32), -5.0, 5.0)
    return fresh.astype(jnp.bfloat16)


def steps_of(key, shape, split, smallest, top_value):
    gain = 1.0
    for dim, parts in split:
        steps = jax.random.uniform(jax.random.fold_in(jax.random.fold_in(key, 6), dim), (parts,), jnp.float32, smallest / len(split), top_value / len(split))
        gain = gain * jnp.repeat(jnp.exp(steps), shape[dim] // parts).reshape((-1,) + (1,) * (len(shape) - 1 - dim))
    return gain


def profile(number_of, total, limit, skew):
    portions = [(1 << 20) // math.isqrt(rank ** skew) + 1 for rank in range(2, number_of + 1)]
    spare, holding = total - limit - (number_of - 1), [1] * (number_of - 1)
    while spare > 0:
        movable = [i for i in range(number_of - 1) if holding[i] < limit]
        whole, left = sum([portions[i] for i in movable]), spare
        for i in movable:
            addition = min(limit - holding[i], max(1, left * portions[i] // whole), spare)
            holding[i] = holding[i] + addition
            spare = spare - addition
    return np.array([limit] + holding)


def uneven_parts(key, number_of, total, limit, skew):
    if number_of == 2:
        one = jax.random.randint(key, (), max(1, total - limit), min(limit, total - 1) + 1)
        return jnp.stack([one, total - one])
    lengths = jnp.asarray(profile(number_of, total, limit, skew), jnp.int32)
    pairs = (number_of - 1) // 2
    source_of, receiver = lengths[1:1 + 2 * pairs:2], lengths[2:2 + 2 * pairs:2]
    margin = jnp.minimum(source_of - 1, limit - receiver)
    shifted = jax.random.randint(jax.random.fold_in(key, 1), (pairs,), 0, 1 << 20) % (margin + 1)
    lengths = lengths.at[1:1 + 2 * pairs:2].set(source_of - shifted).at[2:2 + 2 * pairs:2].set(receiver + shifted)
    return lengths[jax.random.permutation(jax.random.fold_in(key, 2), number_of)]


def bell_draw(rng, extent, spread, bound, cuts=(), kind=jnp.bfloat16):
    entries = jax.random.normal(rng, extent, jnp.float32) * spread
    if len(cuts) > 0:
        entries = steps_of(rng, extent, cuts, -0.22, 0.18) * entries
    return jnp.clip(entries, min=-bound, max=bound).astype(kind)


def setup_inputs(seed: int = 0, part: int = 0) -> dict:
    splits = jax.random.split(jax.random.key(seed), 7)
    part_keys = jax.random.split(jax.random.fold_in(splits[6], part), 7)
    queries = draw_queries(jax.random.fold_in(jax.random.fold_in(splits[6], part), 71), part)
    keys = draw_keys(jax.random.fold_in(jax.random.fold_in(splits[6], part), 71), part)
    values = bell_draw(part_keys[2], (SEQ, HEADS * HEAD), 1.0, 6.0, ((0, 16),))
    outputs = bell_draw(part_keys[3], (SEQ, HEADS * HEAD), 1.0, 6.0, ((0, 16),))
    out_grad = bell_draw(part_keys[4], (SEQ, HEADS * HEAD), 1.0, 6.0, ((0, 16),))
    segment_ids = jnp.searchsorted(jnp.cumsum(uneven_parts(part_keys[5], DOCS, SEQ, LONGEST, 1)), jnp.arange(SEQ), side="right").astype(jnp.int32)
    return {"queries": queries, "keys": keys, "values": values, "outputs": outputs, "out_grad": out_grad, "segment_ids": segment_ids}


masked_score = -1e30


def reference(queries, keys, values, outputs, out_grad, segment_ids):
    length = queries.shape[0]
    scale = HEAD ** -0.5
    positions = jnp.arange(length)
    offset = positions[:, None] - positions[None, :]
    visible = (offset >= 0) & (offset < WINDOW) & (segment_ids[:, None] == segment_ids[None, :])

    def split_heads(x):
        return x.reshape(length, HEADS, HEAD).transpose(1, 0, 2)

    def head_grads(pieces):
        query, key_part, value_part, output, grad = pieces
        scores = jnp.dot(query, key_part.T, preferred_element_type=jnp.float32) * scale
        scores = jnp.where(visible, scores, masked_score)
        top = jnp.max(scores, axis=1, keepdims=True)
        total = jnp.sum(jnp.exp(scores - top), axis=1, keepdims=True)
        lse = top + jnp.log(total)
        probs = jnp.exp(scores - lse)
        probs_low = probs.astype(jnp.bfloat16)
        delta = jnp.sum(grad.astype(jnp.float32) * output.astype(jnp.float32), axis=1, keepdims=True)
        dprobs = jnp.dot(grad, value_part.T, preferred_element_type=jnp.float32)
        dscores = (probs * (dprobs - delta)).astype(jnp.bfloat16)
        dquery = (jnp.dot(dscores, key_part, preferred_element_type=jnp.float32) * scale).astype(jnp.bfloat16)
        dkey = (jnp.dot(dscores.T, query, preferred_element_type=jnp.float32) * scale).astype(jnp.bfloat16)
        dvalue = jnp.dot(probs_low.T, grad, preferred_element_type=jnp.float32).astype(jnp.bfloat16)
        return dquery, dkey, dvalue

    stacked = (split_heads(queries), split_heads(keys), split_heads(values), split_heads(outputs), split_heads(out_grad))
    dquery, dkey, dvalue = lax.map(head_grads, stacked)

    def join_heads(x):
        return x.transpose(1, 0, 2).reshape(length, HEADS * HEAD)

    return join_heads(dquery), join_heads(dkey), join_heads(dvalue)
```

```python
import jax
import jax.numpy as jnp
from jax import lax
from jax.experimental import pallas as pl
from jax.experimental.pallas import tpu as pltpu
from jax.sharding import PartitionSpec as P

HEAD = 128
WIN = 4
WINDOW = 768
GROUP = 4
LOG2E = 1.4426950408889634
masked_score = -1e30
MESH = pl.DeviceIdType.MESH


def dot(a, b, dims):
    return lax.dot_general(a, b, (dims, ((), ())), preferred_element_type=jnp.float32)


def kernel(
    q_hbm, k_hbm, v_hbm, o_hbm, do_hbm, seg_ref,
    dq_hbm, dk_hbm, dv_hbm,
    qb, dob, kb, vb, ob, dol, segsrc, segs, dsrc, deltas, lows,
    dk_acc, dv_acc, dq_out, dk_out, dv_out, halo_out, halo_in,
    in_send, in_recv, fwd_send, fwd_recv, ret_send, ret_recv, out_send, out_recv,
    seg_send, seg_recv, del_send, del_recv, loc_sem,
):
    rows = q_hbm.shape[0]
    heads = q_hbm.shape[1] // HEAD
    mine = heads // GROUP
    halo = (WIN - 1) * rows
    span = WIN * rows
    scale = HEAD ** (-0.5)
    n_ctx = lax.axis_size("ctx")
    n_x = n_ctx // GROUP
    me = lax.axis_index("ctx")
    x = me // GROUP
    g = lax.rem(me, GROUP)
    y = g // 2
    c = lax.rem(g, 2)
    peers = [2 * (1 - y) + c, 2 * (1 - y) + (1 - c), 2 * y + (1 - c)]
    ahead = lax.rem(x + 1, n_x) * GROUP + g
    behind = lax.rem(x + n_x - 1, n_x) * GROUP + g

    barrier = pltpu.get_barrier_semaphore()
    for other in [x * GROUP + p for p in peers] + [ahead, behind]:
        pl.semaphore_signal(barrier, inc=1, device_id={"ctx": other}, device_id_type=MESH)
    pl.semaphore_wait(barrier, 5)

    def remote(src, dst, send, recv, to):
        return pltpu.make_async_remote_copy(
            src_ref=src, dst_ref=dst, send_sem=send, recv_sem=recv,
            device_id={"ctx": to}, device_id_type=MESH,
        )

    def wait_bytes(ref, sem):
        pltpu.make_async_copy(ref, ref, sem).wait()

    def columns(owner, j):
        return pl.ds(pl.multiple_of((owner * mine + j) * HEAD, HEAD), HEAD)

    def place(block, first):
        return pl.ds(pl.multiple_of(first + block * rows, rows), rows)

    arrays = [(k_hbm, kb, halo), (v_hbm, vb, halo), (q_hbm, qb, 0), (do_hbm, dob, 0)]

    segsrc[...] = jnp.broadcast_to(seg_ref[...], segsrc.shape)
    segs[WIN - 1 + g] = segsrc[...]
    for p in peers:
        remote(segsrc, segs.at[WIN - 1 + g], seg_send.at[0], seg_recv.at[0], x * GROUP + p).start()

    o_copy = pltpu.make_async_copy(o_hbm, ob, loc_sem.at[0])
    do_copy = pltpu.make_async_copy(do_hbm, dol, loc_sem.at[1])
    o_copy.start()
    do_copy.start()

    def start_in(j, carry):
        for a, (src, dst, first) in enumerate(arrays):
            for p in peers:
                remote(
                    src.at[:, columns(p, j)], dst.at[j, place(g, first)],
                    in_send.at[j, a], in_recv.at[j, a], x * GROUP + p,
                ).start()
            pltpu.make_async_copy(
                src.at[:, columns(g, j)], dst.at[j, place(g, first)], in_recv.at[j, a]
            ).start()
        return carry

    lax.fori_loop(0, mine, start_in, 0)

    o_copy.wait()
    do_copy.wait()

    def one_delta(h, carry):
        cols = pl.ds(pl.multiple_of(h * HEAD, HEAD), HEAD)
        product = ob[:, cols].astype(jnp.float32) * dol[:, cols].astype(jnp.float32)
        dsrc[h // mine, pl.ds(lax.rem(h, mine), 1), :] = jnp.sum(product.T, axis=0, keepdims=True)
        return carry

    lax.fori_loop(0, heads, one_delta, 0)
    deltas[g] = dsrc[g]
    for p in peers:
        remote(dsrc.at[p], deltas.at[g], del_send.at[0], del_recv.at[0], x * GROUP + p).start()

    wait_bytes(segs.at[0 : GROUP - 1], seg_recv.at[0])
    seg_fwd = remote(segs.at[WIN:], segs.at[0 : WIN - 1], seg_send.at[1], seg_recv.at[1], ahead)
    seg_fwd.start()
    seg_fwd.wait_recv()
    seg_fwd.wait_send()
    for b in range(GROUP):
        ids = segs[WIN - 1 + b][0:1, :]
        low = lax.broadcasted_iota(jnp.int32, (1, rows), 1) + (span - rows - WINDOW + 1)
        first = jnp.zeros((1, rows), jnp.int32)
        for w in range(b, b + WIN):
            theirs = segs[w][0:1, :]
            if w < WIN - 1:
                theirs = jnp.where(x == 0, -1, theirs)
            for doc in range(8):
                fewer = jnp.sum((theirs < doc).astype(jnp.int32), axis=1, keepdims=True)
                first = first + jnp.where(ids == doc, fewer, 0)
        lows[b] = jnp.broadcast_to(jnp.maximum(low, first), (8, rows))
    wait_bytes(deltas.at[0 : GROUP - 1], del_recv.at[0])

    def compute(j):
        dk_acc[j] = jnp.zeros(dk_acc.shape[1:], jnp.float32)
        dv_acc[j] = jnp.zeros(dv_acc.shape[1:], jnp.float32)

        def block(b, carry):
            window = pl.ds(pl.multiple_of(b * rows, rows), span)
            own = pl.ds(pl.multiple_of(b * rows, rows), rows)
            query, grad = qb[j, own, :], dob[j, own, :]
            key, value = kb[j, window, :], vb[j, window, :]
            place_k = lax.broadcasted_iota(jnp.int32, (span, rows), 0)
            place_q = lax.broadcasted_iota(jnp.int32, (span, rows), 1) + halo
            visible = (place_k <= place_q) & (place_k >= lows[b][0:1, :])
            scores = dot(key, query, ((1,), (1,))) * (scale * LOG2E)
            scores = jnp.where(visible, scores, masked_score)
            top = jnp.max(scores, axis=0, keepdims=True)
            weights = jnp.exp2(scores - top)
            total = jnp.sum(weights, axis=0, keepdims=True)
            probs = weights * (1.0 / total)
            probs_low = probs.astype(jnp.bfloat16)
            dv_acc[j, window, :] += dot(probs_low, grad, ((1,), (0,)))
            dprobs = dot(value, grad, ((1,), (1,)))
            delta = deltas[b, pl.ds(j, 1), :]
            dscores = (probs * (dprobs - delta)).astype(jnp.bfloat16)
            dk_acc[j, window, :] += dot(dscores, query, ((1,), (0,)))
            dq_out[j, own, :] = (dot(dscores, key, ((0,), (0,))) * scale).astype(jnp.bfloat16)
            return carry

        lax.fori_loop(0, GROUP, block, 0)

    def send_out(j, a, src, dst):
        for p in peers:
            remote(
                src.at[j, place(p, 0)], dst.at[:, columns(g, j)],
                out_send.at[j, a], out_recv.at[j, a], x * GROUP + p,
            ).start()
        pltpu.make_async_copy(
            src.at[j, place(g, 0)], dst.at[:, columns(g, j)], out_recv.at[j, a]
        ).start()

    def forward(j, a, buf):
        return remote(
            buf.at[j, span : span + halo], buf.at[j, 0:halo],
            fwd_send.at[j, a], fwd_recv.at[j, a], ahead,
        )

    def give_back(j, a):
        return remote(
            halo_out.at[a, j], halo_in.at[a, j], ret_send.at[j, a], ret_recv.at[j, a], behind
        )

    def step(t, carry):
        @pl.when(t < mine)
        def _():
            for a, buf in enumerate((kb, vb)):
                wait_bytes(buf.at[t, halo:], in_recv.at[t, a])
                forward(t, a, buf).start()

        @pl.when((t >= 1) & (t <= mine))
        def _():
            j = t - 1
            for a, buf in enumerate((qb, dob)):
                wait_bytes(buf.at[j], in_recv.at[j, 2 + a])
            for a, buf in enumerate((kb, vb)):
                forward(j, a, buf).wait_recv()
            compute(j)
            send_out(j, 0, dq_out, dq_hbm)
            halo_out[0, j] = (dk_acc[j, 0:halo, :] * scale).astype(jnp.bfloat16)
            halo_out[1, j] = dv_acc[j, 0:halo, :].astype(jnp.bfloat16)
            for a in range(2):
                give_back(j, a).start()

        @pl.when(t >= 2)
        def _():
            j = t - 2
            for a, (acc, out, dst, factor) in enumerate(
                ((dk_acc, dk_out, dk_hbm, scale), (dv_acc, dv_out, dv_hbm, 1.0))
            ):
                give_back(j, a).wait_recv()
                out[j, 0:rows, :] = (acc[j, halo:span, :] * factor).astype(jnp.bfloat16)
                out[j, rows:, :] = (
                    acc[j, span:, :] * factor + halo_in[a, j].astype(jnp.float32)
                ).astype(jnp.bfloat16)
                send_out(j, 1 + a, out, dst)

        return carry

    lax.fori_loop(0, mine + 2, step, 0)

    wait_bytes(segs.at[0 : GROUP - 1], seg_send.at[0])
    wait_bytes(deltas.at[0 : GROUP - 1], del_send.at[0])

    def drain(j, carry):
        for a in range(4):
            wait_bytes(qb.at[j, 0 : (GROUP - 1) * rows], in_send.at[j, a])
        for a, buf in enumerate((kb, vb)):
            forward(j, a, buf).wait_send()
            give_back(j, a).wait_send()
        for a in range(3):
            wait_bytes(dq_out.at[j, 0 : (GROUP - 1) * rows], out_send.at[j, a])
            wait_bytes(dq_out.at[j], out_recv.at[j, a])
        return carry

    lax.fori_loop(0, mine, drain, 0)


def body(queries, keys, values, outputs, out_grad, segment_ids):
    rows, width = queries.shape
    mine = width // HEAD // GROUP
    halo, group = (WIN - 1) * rows, GROUP * rows
    bf16, f32, i32 = jnp.bfloat16, jnp.float32, jnp.int32
    dma = pltpu.SemaphoreType.DMA
    anywhere = pl.BlockSpec(memory_space=pl.ANY)
    return pl.pallas_call(
        kernel,
        out_shape=[jax.ShapeDtypeStruct((rows, width), bf16)] * 3,
        in_specs=[anywhere] * 5 + [pl.BlockSpec(memory_space=pltpu.VMEM)],
        out_specs=[anywhere] * 3,
        scratch_shapes=[
            pltpu.VMEM((mine, group, HEAD), bf16),
            pltpu.VMEM((mine, group, HEAD), bf16),
            pltpu.VMEM((mine, halo + group, HEAD), bf16),
            pltpu.VMEM((mine, halo + group, HEAD), bf16),
            pltpu.VMEM((rows, width), bf16),
            pltpu.VMEM((rows, width), bf16),
            pltpu.VMEM((8, rows), i32),
            pltpu.VMEM((WIN - 1 + GROUP, 8, rows), i32),
            pltpu.VMEM((GROUP, 8, rows), f32),
            pltpu.VMEM((GROUP, 8, rows), f32),
            pltpu.VMEM((GROUP, 8, rows), i32),
            pltpu.VMEM((mine, halo + group, HEAD), f32),
            pltpu.VMEM((mine, halo + group, HEAD), f32),
            pltpu.VMEM((mine, group, HEAD), bf16),
            pltpu.VMEM((mine, group, HEAD), bf16),
            pltpu.VMEM((mine, group, HEAD), bf16),
            pltpu.VMEM((2, mine, halo, HEAD), bf16),
            pltpu.VMEM((2, mine, halo, HEAD), bf16),
            dma((mine, 4)), dma((mine, 4)),
            dma((mine, 2)), dma((mine, 2)),
            dma((mine, 2)), dma((mine, 2)),
            dma((mine, 3)), dma((mine, 3)),
            dma((2,)), dma((2,)),
            dma((1,)), dma((1,)),
            dma((2,)),
        ],
        compiler_params=pltpu.CompilerParams(
            collective_id=0, has_side_effects=True, vmem_limit_bytes=48 * 1024 * 1024
        ),
        name="window_attention_grads",
    )(queries, keys, values, outputs, out_grad, segment_ids.reshape(1, rows))


def solution(mesh):
    part = P(("dp", "ctx"), None)
    return jax.shard_map(
        body,
        mesh=mesh,
        in_specs=(part, part, part, part, part, P(("dp", "ctx"))),
        out_specs=(part, part, part),
        check_vma=False,
    )
```

```python
import jax
import jax.numpy as jnp
from jax import lax
from jax.experimental import pallas as pl
from jax.experimental.pallas import tpu as pltpu
from jax.sharding import PartitionSpec as P

HEAD = 128
WIN = 4
WINDOW = 768
GROUP = 4
LOG2E = 1.4426950408889634
masked_score = -1e30
MESH = pl.DeviceIdType.MESH


def dot(a, b, dims):
    return lax.dot_general(a, b, (dims, ((), ())), preferred_element_type=jnp.float32)


def kernel(
    q_hbm, k_hbm, v_hbm, o_hbm, do_hbm, seg_ref,
    dq_hbm, dk_hbm, dv_hbm,
    qb, dob, kb, vb, ob, dol, segsrc, segs, dsrc, deltas, lows,
    dk_acc, dv_acc, dq_out, dk_out, dv_out, halo_out, halo_in,
    in_send, in_recv, fwd_send, fwd_recv, ret_send, ret_recv, out_send, out_recv,
    seg_send, seg_recv, del_send, del_recv, loc_sem,
):
    rows = q_hbm.shape[0]
    heads = q_hbm.shape[1] // HEAD
    mine = heads // GROUP
    halo = (WIN - 1) * rows
    span = WIN * rows
    scale = HEAD ** (-0.5)
    n_ctx = lax.axis_size("ctx")
    n_x = n_ctx // GROUP
    me = lax.axis_index("ctx")
    x = me // GROUP
    g = lax.rem(me, GROUP)
    y = g // 2
    c = lax.rem(g, 2)
    peers = [2 * (1 - y) + c, 2 * (1 - y) + (1 - c), 2 * y + (1 - c)]
    ahead = lax.rem(x + 1, n_x) * GROUP + g
    behind = lax.rem(x + n_x - 1, n_x) * GROUP + g

    barrier = pltpu.get_barrier_semaphore()
    for other in [x * GROUP + p for p in peers] + [ahead, behind]:
        pl.semaphore_signal(barrier, inc=1, device_id={"ctx": other}, device_id_type=MESH)
    pl.semaphore_wait(barrier, 5)

    def remote(src, dst, send, recv, to):
        return pltpu.make_async_remote_copy(
            src_ref=src, dst_ref=dst, send_sem=send, recv_sem=recv,
            device_id={"ctx": to}, device_id_type=MESH,
        )

    def wait_bytes(ref, sem):
        pltpu.make_async_copy(ref, ref, sem).wait()

    def columns(owner, j):
        return pl.ds(pl.multiple_of((owner * mine + j) * HEAD, HEAD), HEAD)

    def place(block, first):
        return pl.ds(pl.multiple_of(first + block * rows, rows), rows)

    arrays = [(k_hbm, kb, halo), (v_hbm, vb, halo), (q_hbm, qb, 0), (do_hbm, dob, 0)]

    segsrc[...] = jnp.broadcast_to(seg_ref[...], segsrc.shape)
    segs[WIN - 1 + g] = segsrc[...]
    for p in peers:
        remote(segsrc, segs.at[WIN - 1 + g], seg_send.at[0], seg_recv.at[0], x * GROUP + p).start()

    o_copy = pltpu.make_async_copy(o_hbm, ob, loc_sem.at[0])
    do_copy = pltpu.make_async_copy(do_hbm, dol, loc_sem.at[1])
    o_copy.start()
    do_copy.start()

    def start_in(j, stage):
        for a in range(2 * stage, 2 * stage + 2):
            src, dst, first = arrays[a]
            for p in peers:
                remote(
                    src.at[:, columns(p, j)], dst.at[j, place(g, first)],
                    in_send.at[j, a], in_recv.at[j, a], x * GROUP + p,
                ).start()
            pltpu.make_async_copy(
                src.at[:, columns(g, j)], dst.at[j, place(g, first)], in_recv.at[j, a]
            ).start()

    def wait_in(j, stage):
        for a in range(2 * stage, 2 * stage + 2):
            _, dst, first = arrays[a]
            wait_bytes(dst.at[j, first:], in_recv.at[j, a])
            wait_bytes(dst.at[j, 0 : (GROUP - 1) * rows], in_send.at[j, a])

    start_in(0, 0)
    start_in(0, 1)

    o_copy.wait()
    do_copy.wait()

    def one_delta(h, carry):
        cols = pl.ds(pl.multiple_of(h * HEAD, HEAD), HEAD)
        product = ob[:, cols].astype(jnp.float32) * dol[:, cols].astype(jnp.float32)
        dsrc[h // mine, pl.ds(lax.rem(h, mine), 1), :] = jnp.sum(product.T, axis=0, keepdims=True)
        return carry

    lax.fori_loop(0, heads, one_delta, 0)
    deltas[g] = dsrc[g]
    for p in peers:
        remote(dsrc.at[p], deltas.at[g], del_send.at[0], del_recv.at[0], x * GROUP + p).start()

    wait_bytes(segs.at[0 : GROUP - 1], seg_recv.at[0])
    seg_fwd = remote(segs.at[WIN:], segs.at[0 : WIN - 1], seg_send.at[1], seg_recv.at[1], ahead)
    seg_fwd.start()
    seg_fwd.wait_recv()
    seg_fwd.wait_send()
    for b in range(GROUP):
        ids = segs[WIN - 1 + b][0:1, :]
        low = lax.broadcasted_iota(jnp.int32, (1, rows), 1) + (span - rows - WINDOW + 1)
        first = jnp.zeros((1, rows), jnp.int32)
        for w in range(b, b + WIN):
            theirs = segs[w][0:1, :]
            if w < WIN - 1:
                theirs = jnp.where(x == 0, -1, theirs)
            for doc in range(8):
                fewer = jnp.sum((theirs < doc).astype(jnp.int32), axis=1, keepdims=True)
                first = first + jnp.where(ids == doc, fewer, 0)
        lows[b] = jnp.broadcast_to(jnp.maximum(low, first), (8, rows))
    wait_bytes(deltas.at[0 : GROUP - 1], del_recv.at[0])

    def compute(j):
        dk_acc[j] = jnp.zeros(dk_acc.shape[1:], jnp.float32)
        dv_acc[j] = jnp.zeros(dv_acc.shape[1:], jnp.float32)

        def block(b, carry):
            window = pl.ds(pl.multiple_of(b * rows, rows), span)
            own = pl.ds(pl.multiple_of(b * rows, rows), rows)
            query, grad = qb[j, own, :], dob[j, own, :]
            key, value = kb[j, window, :], vb[j, window, :]
            place_k = lax.broadcasted_iota(jnp.int32, (span, rows), 0)
            place_q = lax.broadcasted_iota(jnp.int32, (span, rows), 1) + halo
            visible = (place_k <= place_q) & (place_k >= lows[b][0:1, :])
            scores = dot(key, query, ((1,), (1,))) * (scale * LOG2E)
            scores = jnp.where(visible, scores, masked_score)
            top = jnp.max(scores, axis=0, keepdims=True)
            weights = jnp.exp2(scores - top)
            total = jnp.sum(weights, axis=0, keepdims=True)
            probs = weights * (1.0 / total)
            probs_low = probs.astype(jnp.bfloat16)
            dv_acc[j, window, :] += dot(probs_low, grad, ((1,), (0,)))
            dprobs = dot(value, grad, ((1,), (1,)))
            delta = deltas[b, pl.ds(j, 1), :]
            dscores = (probs * (dprobs - delta)).astype(jnp.bfloat16)
            dk_acc[j, window, :] += dot(dscores, query, ((1,), (0,)))
            dq_out[j, own, :] = (dot(dscores, key, ((0,), (0,))) * scale).astype(jnp.bfloat16)
            return carry

        lax.fori_loop(0, GROUP, block, 0)

    def send_out(j, a, src, dst):
        for p in peers:
            remote(
                src.at[j, place(p, 0)], dst.at[:, columns(g, j)],
                out_send.at[j, a], out_recv.at[j, a], x * GROUP + p,
            ).start()
        pltpu.make_async_copy(
            src.at[j, place(g, 0)], dst.at[:, columns(g, j)], out_recv.at[j, a]
        ).start()

    def forward(j, a, buf):
        return remote(
            buf.at[j, span : span + halo], buf.at[j, 0:halo],
            fwd_send.at[j, a], fwd_recv.at[j, a], ahead,
        )

    def give_back(j, a):
        return remote(
            halo_out.at[a, j], halo_in.at[a, j], ret_send.at[j, a], ret_recv.at[j, a], behind
        )

    def finish(j):
        for a, (acc, out, factor) in enumerate(((dk_acc, dk_out, scale), (dv_acc, dv_out, 1.0))):
            give_back(j, a).wait_recv()
            out[j, 0:rows, :] = (acc[j, halo:span, :] * factor).astype(jnp.bfloat16)
            out[j, rows:, :] = (
                acc[j, span:, :] * factor + halo_in[a, j].astype(jnp.float32)
            ).astype(jnp.bfloat16)

    def send_key_value(j):
        send_out(j, 1, dk_out, dk_hbm)
        send_out(j, 2, dv_out, dv_hbm)

    last = mine - 1

    def step(t, carry):
        @pl.when(t < mine)
        def _():
            wait_in(t, 0)
            for a, buf in enumerate((kb, vb)):
                forward(t, a, buf).start()

        @pl.when(t < last)
        def _():
            start_in(t + 1, 0)

        @pl.when(t == last)
        def _():
            def late(j, carry):
                send_out(j, 0, dq_out, dq_hbm)
                return carry

            lax.fori_loop(0, last - 1, late, 0)

        @pl.when((t >= 1) & (t <= mine))
        def _():
            j = t - 1
            for a, buf in enumerate((kb, vb)):
                forward(j, a, buf).wait_recv()
            compute(j)
            halo_out[0, j] = (dk_acc[j, 0:halo, :] * scale).astype(jnp.bfloat16)
            halo_out[1, j] = dv_acc[j, 0:halo, :].astype(jnp.bfloat16)
            for a in range(2):
                give_back(j, a).start()

            @pl.when(t >= last)
            def _():
                send_out(j, 0, dq_out, dq_hbm)

        @pl.when(t < mine)
        def _():
            wait_in(t, 1)

        @pl.when(t < last)
        def _():
            start_in(t + 1, 1)

        @pl.when(t >= 2)
        def _():
            finish(t - 2)

        @pl.when(t == last)
        def _():
            def late(j, carry):
                send_key_value(j)
                return carry

            lax.fori_loop(0, last - 2, late, 0)

        @pl.when(t >= last)
        def _():
            send_key_value(t - 2)

        return carry

    lax.fori_loop(0, mine + 2, step, 0)

    wait_bytes(segs.at[0 : GROUP - 1], seg_send.at[0])
    wait_bytes(deltas.at[0 : GROUP - 1], del_send.at[0])

    def drain(j, carry):
        for a, buf in enumerate((kb, vb)):
            forward(j, a, buf).wait_send()
            give_back(j, a).wait_send()
        for a in range(3):
            wait_bytes(dq_out.at[j, 0 : (GROUP - 1) * rows], out_send.at[j, a])
            wait_bytes(dq_out.at[j], out_recv.at[j, a])
        return carry

    lax.fori_loop(0, mine, drain, 0)


def body(queries, keys, values, outputs, out_grad, segment_ids):
    rows, width = queries.shape
    mine = width // HEAD // GROUP
    halo, group = (WIN - 1) * rows, GROUP * rows
    bf16, f32, i32 = jnp.bfloat16, jnp.float32, jnp.int32
    dma = pltpu.SemaphoreType.DMA
    anywhere = pl.BlockSpec(memory_space=pltpu.HBM)
    return pl.pallas_call(
        kernel,
        out_shape=[jax.ShapeDtypeStruct((rows, width), bf16)] * 3,
        in_specs=[anywhere] * 5 + [pl.BlockSpec(memory_space=pltpu.VMEM)],
        out_specs=[anywhere] * 3,
        scratch_shapes=[
            pltpu.VMEM((mine, group, HEAD), bf16),
            pltpu.VMEM((mine, group, HEAD), bf16),
            pltpu.VMEM((mine, halo + group, HEAD), bf16),
            pltpu.VMEM((mine, halo + group, HEAD), bf16),
            pltpu.VMEM((rows, width), bf16),
            pltpu.VMEM((rows, width), bf16),
            pltpu.VMEM((8, rows), i32),
            pltpu.VMEM((WIN - 1 + GROUP, 8, rows), i32),
            pltpu.VMEM((GROUP, 8, rows), f32),
            pltpu.VMEM((GROUP, 8, rows), f32),
            pltpu.VMEM((GROUP, 8, rows), i32),
            pltpu.VMEM((mine, halo + group, HEAD), f32),
            pltpu.VMEM((mine, halo + group, HEAD), f32),
            pltpu.VMEM((mine, group, HEAD), bf16),
            pltpu.VMEM((mine, group, HEAD), bf16),
            pltpu.VMEM((mine, group, HEAD), bf16),
            pltpu.VMEM((2, mine, halo, HEAD), bf16),
            pltpu.VMEM((2, mine, halo, HEAD), bf16),
            dma((mine, 4)), dma((mine, 4)),
            dma((mine, 2)), dma((mine, 2)),
            dma((mine, 2)), dma((mine, 2)),
            dma((mine, 3)), dma((mine, 3)),
            dma((2,)), dma((2,)),
            dma((1,)), dma((1,)),
            dma((2,)),
        ],
        compiler_params=pltpu.CompilerParams(
            collective_id=0, has_side_effects=True, vmem_limit_bytes=62 * 1024 * 1024
        ),
        name="window_attention_grads",
    )(queries, keys, values, outputs, out_grad, segment_ids.reshape(1, rows))


def solution(mesh):
    part = P(("dp", "ctx"), None)
    return jax.shard_map(
        body,
        mesh=mesh,
        in_specs=(part, part, part, part, part, P(("dp", "ctx"))),
        out_specs=(part, part, part),
        check_vma=False,
    )
```

```python
import jax
import jax.numpy as jnp
from jax import lax
from jax.experimental import pallas as pl
from jax.experimental.pallas import tpu as pltpu
from jax.sharding import PartitionSpec as P

HEAD = 128
WIN = 4
WINDOW = 768
GROUP = 4
LOG2E = 1.4426950408889634
masked_score = -1e30
MESH = pl.DeviceIdType.MESH


def dot(a, b, dims):
    return lax.dot_general(a, b, (dims, ((), ())), preferred_element_type=jnp.float32)


def kernel(
    q_hbm, k_hbm, v_hbm, o_hbm, do_hbm, seg_ref,
    dq_hbm, dk_hbm, dv_hbm,
    qb, dob, kb, vb, ob, dol, segsrc, segs, dsrc, deltas, lows,
    dk_acc, dv_acc, dq_out, dk_out, dv_out, halo_out, halo_in,
    in_send, in_recv, fwd_send, fwd_recv, ret_send, ret_recv, out_send, out_recv,
    seg_send, seg_recv, del_send, del_recv, loc_sem,
):
    rows = q_hbm.shape[0]
    heads = q_hbm.shape[1] // HEAD
    mine = heads // GROUP
    halo = (WIN - 1) * rows
    span = WIN * rows
    scale = HEAD ** (-0.5)
    n_ctx = lax.axis_size("ctx")
    n_x = n_ctx // GROUP
    me = lax.axis_index("ctx")
    x = me // GROUP
    g = lax.rem(me, GROUP)
    y = g // 2
    c = lax.rem(g, 2)
    peers = [2 * (1 - y) + c, 2 * (1 - y) + (1 - c), 2 * y + (1 - c)]
    ahead = lax.rem(x + 1, n_x) * GROUP + g
    behind = lax.rem(x + n_x - 1, n_x) * GROUP + g

    barrier = pltpu.get_barrier_semaphore()
    for other in [x * GROUP + p for p in peers] + [ahead, behind]:
        pl.semaphore_signal(barrier, inc=1, device_id={"ctx": other}, device_id_type=MESH)
    pl.semaphore_wait(barrier, 5)

    def remote(src, dst, send, recv, to):
        return pltpu.make_async_remote_copy(
            src_ref=src, dst_ref=dst, send_sem=send, recv_sem=recv,
            device_id={"ctx": to}, device_id_type=MESH,
        )

    def wait_bytes(ref, sem):
        pltpu.make_async_copy(ref, ref, sem).wait()

    def columns(owner, j):
        return pl.ds(pl.multiple_of((owner * mine + j) * HEAD, HEAD), HEAD)

    def place(block, first):
        return pl.ds(pl.multiple_of(first + block * rows, rows), rows)

    arrays = [(k_hbm, kb, halo), (v_hbm, vb, halo), (q_hbm, qb, 0), (do_hbm, dob, 0)]

    segsrc[...] = jnp.broadcast_to(seg_ref[...], segsrc.shape)
    segs[WIN - 1 + g] = segsrc[...]
    for p in peers:
        remote(segsrc, segs.at[WIN - 1 + g], seg_send.at[0], seg_recv.at[0], x * GROUP + p).start()

    o_copy = pltpu.make_async_copy(o_hbm, ob, loc_sem.at[0])
    do_copy = pltpu.make_async_copy(do_hbm, dol, loc_sem.at[1])
    o_copy.start()
    do_copy.start()

    def start_in(j, stage):
        for a in range(2 * stage, 2 * stage + 2):
            src, dst, first = arrays[a]
            for p in peers:
                remote(
                    src.at[:, columns(p, j)], dst.at[j, place(g, first)],
                    in_send.at[j, a], in_recv.at[j, a], x * GROUP + p,
                ).start()
            pltpu.make_async_copy(
                src.at[:, columns(g, j)], dst.at[j, place(g, first)], in_recv.at[j, a]
            ).start()

    def wait_in(j, stage):
        for a in range(2 * stage, 2 * stage + 2):
            _, dst, first = arrays[a]
            wait_bytes(dst.at[j, first:], in_recv.at[j, a])
            wait_bytes(dst.at[j, 0 : (GROUP - 1) * rows], in_send.at[j, a])

    start_in(0, 0)
    start_in(0, 1)

    o_copy.wait()
    do_copy.wait()

    def one_delta(h, carry):
        cols = pl.ds(pl.multiple_of(h * HEAD, HEAD), HEAD)
        product = ob[:, cols].astype(jnp.float32) * dol[:, cols].astype(jnp.float32)
        dsrc[h // mine, pl.ds(lax.rem(h, mine), 1), :] = jnp.sum(product.T, axis=0, keepdims=True)
        return carry

    lax.fori_loop(0, heads, one_delta, 0)
    deltas[g] = dsrc[g]
    for p in peers:
        remote(dsrc.at[p], deltas.at[g], del_send.at[0], del_recv.at[0], x * GROUP + p).start()

    wait_bytes(segs.at[0 : GROUP - 1], seg_recv.at[0])
    seg_fwd = remote(segs.at[WIN:], segs.at[0 : WIN - 1], seg_send.at[1], seg_recv.at[1], ahead)
    seg_fwd.start()
    seg_fwd.wait_recv()
    seg_fwd.wait_send()
    for b in range(GROUP):
        ids = segs[WIN - 1 + b][0:1, :]
        low = lax.broadcasted_iota(jnp.int32, (1, rows), 1) + (span - rows - WINDOW + 1)
        first = jnp.zeros((1, rows), jnp.int32)
        for w in range(b, b + WIN):
            theirs = segs[w][0:1, :]
            if w < WIN - 1:
                theirs = jnp.where(x == 0, -1, theirs)
            for doc in range(8):
                fewer = jnp.sum((theirs < doc).astype(jnp.int32), axis=1, keepdims=True)
                first = first + jnp.where(ids == doc, fewer, 0)
        lows[b] = jnp.broadcast_to(jnp.maximum(low, first), (8, rows))
    wait_bytes(deltas.at[0 : GROUP - 1], del_recv.at[0])

    def compute(j):
        dk_acc[j] = jnp.zeros(dk_acc.shape[1:], jnp.float32)
        dv_acc[j] = jnp.zeros(dv_acc.shape[1:], jnp.float32)

        def block(b, carry):
            window = pl.ds(pl.multiple_of(b * rows, rows), span)
            own = pl.ds(pl.multiple_of(b * rows, rows), rows)
            query, grad = qb[j, own, :], dob[j, own, :]
            key, value = kb[j, window, :], vb[j, window, :]
            place_k = lax.broadcasted_iota(jnp.int32, (span, rows), 0)
            place_q = lax.broadcasted_iota(jnp.int32, (span, rows), 1) + halo
            visible = (place_k <= place_q) & (place_k >= lows[b][0:1, :])
            scores = dot(key, query, ((1,), (1,))) * (scale * LOG2E)
            scores = jnp.where(visible, scores, masked_score)
            top = jnp.max(scores, axis=0, keepdims=True)
            weights = jnp.exp2(scores - top)
            total = jnp.sum(weights, axis=0, keepdims=True)
            probs = weights * (1.0 / total)
            probs_low = probs.astype(jnp.bfloat16)
            dv_acc[j, window, :] += dot(probs_low, grad, ((1,), (0,)))
            dprobs = dot(value, grad, ((1,), (1,)))
            delta = deltas[b, pl.ds(j, 1), :]
            dscores = (probs * (dprobs - delta)).astype(jnp.bfloat16)
            dk_acc[j, window, :] += dot(dscores, query, ((1,), (0,)))
            dq_out[j, own, :] = (dot(dscores, key, ((0,), (0,))) * scale).astype(jnp.bfloat16)
            return carry

        lax.fori_loop(0, GROUP, block, 0)

    def send_out(j, a, src, dst):
        for p in peers:
            remote(
                src.at[j, place(p, 0)], dst.at[:, columns(g, j)],
                out_send.at[j, a], out_recv.at[j, a], x * GROUP + p,
            ).start()
        pltpu.make_async_copy(
            src.at[j, place(g, 0)], dst.at[:, columns(g, j)], out_recv.at[j, a]
        ).start()

    def forward(j, a, buf):
        return remote(
            buf.at[j, span : span + halo], buf.at[j, 0:halo],
            fwd_send.at[j, a], fwd_recv.at[j, a], ahead,
        )

    def give_back(j, a):
        return remote(
            halo_out.at[a, j], halo_in.at[a, j], ret_send.at[j, a], ret_recv.at[j, a], behind
        )

    def finish(j):
        for a, (acc, out, factor) in enumerate(((dk_acc, dk_out, scale), (dv_acc, dv_out, 1.0))):
            give_back(j, a).wait_recv()
            out[j, 0:rows, :] = (acc[j, halo:span, :] * factor).astype(jnp.bfloat16)
            out[j, rows:, :] = (
                acc[j, span:, :] * factor + halo_in[a, j].astype(jnp.float32)
            ).astype(jnp.bfloat16)

    def send_key_value(j):
        send_out(j, 1, dk_out, dk_hbm)
        send_out(j, 2, dv_out, dv_hbm)

    last = mine - 1

    def step(t, carry):
        @pl.when(t < mine)
        def _():
            wait_in(t, 0)
            for a, buf in enumerate((kb, vb)):
                forward(t, a, buf).start()

        @pl.when(t < last)
        def _():
            start_in(t + 1, 0)

        @pl.when(t == last)
        def _():
            def late(j, carry):
                send_out(j, 0, dq_out, dq_hbm)
                return carry

            lax.fori_loop(0, last - 1, late, 0)

        @pl.when((t >= 1) & (t <= mine))
        def _():
            j = t - 1
            for a, buf in enumerate((kb, vb)):
                forward(j, a, buf).wait_recv()
            compute(j)
            halo_out[0, j] = (dk_acc[j, 0:halo, :] * scale).astype(jnp.bfloat16)
            halo_out[1, j] = dv_acc[j, 0:halo, :].astype(jnp.bfloat16)
            for a in range(2):
                give_back(j, a).start()

            @pl.when(t >= last)
            def _():
                send_out(j, 0, dq_out, dq_hbm)

        @pl.when(t < mine)
        def _():
            wait_in(t, 1)

        @pl.when(t < last)
        def _():
            start_in(t + 1, 1)

        @pl.when(t >= 2)
        def _():
            finish(t - 2)

        @pl.when(t == last)
        def _():
            def late(j, carry):
                send_key_value(j)
                return carry

            lax.fori_loop(0, last - 2, late, 0)

        @pl.when(t >= last)
        def _():
            send_key_value(t - 2)

        return carry

    lax.fori_loop(0, mine + 2, step, 0)

    wait_bytes(segs.at[0 : GROUP - 1], seg_send.at[0])
    wait_bytes(deltas.at[0 : GROUP - 1], del_send.at[0])

    def drain(j, carry):
        for a, buf in enumerate((kb, vb)):
            forward(j, a, buf).wait_send()
            give_back(j, a).wait_send()
        for a in range(3):
            wait_bytes(dq_out.at[j, 0 : (GROUP - 1) * rows], out_send.at[j, a])
            wait_bytes(dq_out.at[j], out_recv.at[j, a])
        return carry

    lax.fori_loop(0, mine, drain, 0)


def body(queries, keys, values, outputs, out_grad, segment_ids):
    rows, width = queries.shape
    mine = width // HEAD // GROUP
    halo, group = (WIN - 1) * rows, GROUP * rows
    bf16, f32, i32 = jnp.bfloat16, jnp.float32, jnp.int32
    dma = pltpu.SemaphoreType.DMA
    anywhere = pl.BlockSpec(memory_space=pltpu.HBM)
    return pl.pallas_call(
        kernel,
        out_shape=[jax.ShapeDtypeStruct((rows, width), bf16)] * 3,
        in_specs=[anywhere] * 5 + [pl.BlockSpec(memory_space=pltpu.VMEM)],
        out_specs=[anywhere] * 3,
        scratch_shapes=[
            pltpu.VMEM((mine, group, HEAD), bf16),
            pltpu.VMEM((mine, group, HEAD), bf16),
            pltpu.VMEM((mine, halo + group, HEAD), bf16),
            pltpu.VMEM((mine, halo + group, HEAD), bf16),
            pltpu.VMEM((rows, width), bf16),
            pltpu.VMEM((rows, width), bf16),
            pltpu.VMEM((8, rows), i32),
            pltpu.VMEM((WIN - 1 + GROUP, 8, rows), i32),
            pltpu.VMEM((GROUP, 8, rows), f32),
            pltpu.VMEM((GROUP, 8, rows), f32),
            pltpu.VMEM((GROUP, 8, rows), i32),
            pltpu.VMEM((mine, halo + group, HEAD), f32),
            pltpu.VMEM((mine, halo + group, HEAD), f32),
            pltpu.VMEM((mine, group, HEAD), bf16),
            pltpu.VMEM((mine, group, HEAD), bf16),
            pltpu.VMEM((mine, group, HEAD), bf16),
            pltpu.VMEM((2, mine, halo, HEAD), bf16),
            pltpu.VMEM((2, mine, halo, HEAD), bf16),
            dma((mine, 4)), dma((mine, 4)),
            dma((mine, 2)), dma((mine, 2)),
            dma((mine, 2)), dma((mine, 2)),
            dma((mine, 3)), dma((mine, 3)),
            dma((2,)), dma((2,)),
            dma((1,)), dma((1,)),
            dma((2,)),
        ],
        compiler_params=pltpu.CompilerParams(
            collective_id=0, has_side_effects=True, vmem_limit_bytes=50 * 1024 * 1024
        ),
        name="window_attention_grads",
    )(queries, keys, values, outputs, out_grad, segment_ids.reshape(1, rows))


def solution(mesh):
    part = P(("dp", "ctx"), None)
    return jax.shard_map(
        body,
        mesh=mesh,
        in_specs=(part, part, part, part, part, P(("dp", "ctx"))),
        out_specs=(part, part, part),
        check_vma=False,
    )
```

```python
import jax
import jax.numpy as jnp
from jax import lax
from jax.experimental import pallas as pl
from jax.experimental.pallas import tpu as pltpu
from jax.sharding import PartitionSpec as P

HEAD = 128
WIN = 4
WINDOW = 768
GROUP = 4
LOG2E = 1.4426950408889634
masked_score = -1e30
MESH = pl.DeviceIdType.MESH


def dot(a, b, dims):
    return lax.dot_general(a, b, (dims, ((), ())), preferred_element_type=jnp.float32)


def kernel(
    q_hbm, k_hbm, v_hbm, o_hbm, do_hbm, seg_hbm,
    dq_hbm, dk_hbm, dv_hbm,
    qb, dob, kb, vb, ob, dol, seg_row, segsrc, segs, dsrc, deltas, lows,
    dk_acc, dv_acc, dq_out, dk_out, dv_out, halo_out, halo_in,
    in_send, in_recv, fwd_send, fwd_recv, ret_send, ret_recv, out_send, out_recv,
    seg_send, seg_recv, del_send, del_recv, loc_sem,
):
    rows = q_hbm.shape[0]
    heads = q_hbm.shape[1] // HEAD
    mine = heads // GROUP
    halo = (WIN - 1) * rows
    span = WIN * rows
    scale = HEAD ** (-0.5)
    n_ctx = lax.axis_size("ctx")
    n_x = n_ctx // GROUP
    me = lax.axis_index("ctx")
    x = me // GROUP
    g = lax.rem(me, GROUP)
    y = g // 2
    c = lax.rem(g, 2)
    peers = [2 * (1 - y) + c, 2 * (1 - y) + (1 - c), 2 * y + (1 - c)]
    ahead = lax.rem(x + 1, n_x) * GROUP + g
    behind = lax.rem(x + n_x - 1, n_x) * GROUP + g

    o_copy = pltpu.make_async_copy(o_hbm, ob, loc_sem.at[0])
    do_copy = pltpu.make_async_copy(do_hbm, dol, loc_sem.at[1])
    seg_copy = pltpu.make_async_copy(seg_hbm, seg_row, loc_sem.at[2])
    seg_copy.start()
    o_copy.start()
    do_copy.start()

    barrier = pltpu.get_barrier_semaphore()
    for other in [x * GROUP + p for p in peers] + [ahead, behind]:
        pl.semaphore_signal(barrier, inc=1, device_id={"ctx": other}, device_id_type=MESH)
    pl.semaphore_wait(barrier, 5)

    def remote(src, dst, send, recv, to):
        return pltpu.make_async_remote_copy(
            src_ref=src, dst_ref=dst, send_sem=send, recv_sem=recv,
            device_id={"ctx": to}, device_id_type=MESH,
        )

    def wait_bytes(ref, sem):
        pltpu.make_async_copy(ref, ref, sem).wait()

    def columns(owner, j):
        return pl.ds(pl.multiple_of((owner * mine + j) * HEAD, HEAD), HEAD)

    def place(block, first):
        return pl.ds(pl.multiple_of(first + block * rows, rows), rows)

    arrays = [(k_hbm, kb, halo), (v_hbm, vb, halo), (q_hbm, qb, 0), (do_hbm, dob, 0)]

    seg_copy.wait()
    segsrc[...] = jnp.broadcast_to(seg_row[...], segsrc.shape)
    segs[WIN - 1 + g] = segsrc[...]
    for p in peers:
        remote(segsrc, segs.at[WIN - 1 + g], seg_send.at[0], seg_recv.at[0], x * GROUP + p).start()

    def start_in(j, stage):
        for a in range(2 * stage, 2 * stage + 2):
            src, dst, first = arrays[a]
            for p in peers:
                remote(
                    src.at[:, columns(p, j)], dst.at[j, place(g, first)],
                    in_send.at[j, a], in_recv.at[j, a], x * GROUP + p,
                ).start()
            pltpu.make_async_copy(
                src.at[:, columns(g, j)], dst.at[j, place(g, first)], in_recv.at[j, a]
            ).start()

    def wait_in(j, stage):
        for a in range(2 * stage, 2 * stage + 2):
            _, dst, first = arrays[a]
            wait_bytes(dst.at[j, first:], in_recv.at[j, a])
            wait_bytes(dst.at[j, 0 : (GROUP - 1) * rows], in_send.at[j, a])

    start_in(0, 0)
    start_in(0, 1)

    o_copy.wait()
    do_copy.wait()

    def one_delta(h, carry):
        cols = pl.ds(pl.multiple_of(h * HEAD, HEAD), HEAD)
        product = ob[:, cols].astype(jnp.float32) * dol[:, cols].astype(jnp.float32)
        dsrc[h // mine, pl.ds(lax.rem(h, mine), 1), :] = jnp.sum(product.T, axis=0, keepdims=True)
        return carry

    lax.fori_loop(0, heads, one_delta, 0)
    deltas[g] = dsrc[g]
    for p in peers:
        remote(dsrc.at[p], deltas.at[g], del_send.at[0], del_recv.at[0], x * GROUP + p).start()

    wait_bytes(segs.at[0 : GROUP - 1], seg_recv.at[0])
    seg_fwd = remote(segs.at[WIN:], segs.at[0 : WIN - 1], seg_send.at[1], seg_recv.at[1], ahead)
    seg_fwd.start()
    seg_fwd.wait_recv()
    seg_fwd.wait_send()
    for b in range(GROUP):
        ids = segs[WIN - 1 + b][0:1, :]
        low = lax.broadcasted_iota(jnp.int32, (1, rows), 1) + (span - rows - WINDOW + 1)
        first = jnp.zeros((1, rows), jnp.int32)
        for w in range(b, b + WIN):
            theirs = segs[w][0:1, :]
            if w < WIN - 1:
                theirs = jnp.where(x == 0, -1, theirs)
            for doc in range(8):
                fewer = jnp.sum((theirs < doc).astype(jnp.int32), axis=1, keepdims=True)
                first = first + jnp.where(ids == doc, fewer, 0)
        lows[b] = jnp.broadcast_to(jnp.maximum(low, first), (8, rows))

    def compute(j):
        dk_acc[j] = jnp.zeros(dk_acc.shape[1:], jnp.float32)
        dv_acc[j] = jnp.zeros(dv_acc.shape[1:], jnp.float32)

        def block(b, carry):
            window = pl.ds(pl.multiple_of(b * rows, rows), span)
            own = pl.ds(pl.multiple_of(b * rows, rows), rows)
            query, grad = qb[j, own, :], dob[j, own, :]
            key, value = kb[j, window, :], vb[j, window, :]
            place_k = lax.broadcasted_iota(jnp.int32, (span, rows), 0)
            place_q = lax.broadcasted_iota(jnp.int32, (span, rows), 1) + halo
            visible = (place_k <= place_q) & (place_k >= lows[b][0:1, :])
            scores = dot(key, query, ((1,), (1,))) * (scale * LOG2E)
            scores = jnp.where(visible, scores, masked_score)
            top = jnp.max(scores, axis=0, keepdims=True)
            weights = jnp.exp2(scores - top)
            total = jnp.sum(weights, axis=0, keepdims=True)
            probs = weights * (1.0 / total)
            probs_low = probs.astype(jnp.bfloat16)
            dv_acc[j, window, :] += dot(probs_low, grad, ((1,), (0,)))
            dprobs = dot(value, grad, ((1,), (1,)))
            delta = deltas[b, pl.ds(j, 1), :]
            dscores = (probs * (dprobs - delta)).astype(jnp.bfloat16)
            dk_acc[j, window, :] += dot(dscores, query, ((1,), (0,)))
            dq_out[j, own, :] = (dot(dscores, key, ((0,), (0,))) * scale).astype(jnp.bfloat16)
            return carry

        lax.fori_loop(0, GROUP, block, 0)

    def send_out(j, a, src, dst):
        for p in peers:
            remote(
                src.at[j, place(p, 0)], dst.at[:, columns(g, j)],
                out_send.at[j, a], out_recv.at[j, a], x * GROUP + p,
            ).start()
        pltpu.make_async_copy(
            src.at[j, place(g, 0)], dst.at[:, columns(g, j)], out_recv.at[j, a]
        ).start()

    def forward(j, a, buf):
        return remote(
            buf.at[j, span : span + halo], buf.at[j, 0:halo],
            fwd_send.at[j, a], fwd_recv.at[j, a], ahead,
        )

    def give_back(j, a):
        return remote(
            halo_out.at[a, j], halo_in.at[a, j], ret_send.at[j, a], ret_recv.at[j, a], behind
        )

    def finish(j):
        for a, (acc, out, factor) in enumerate(((dk_acc, dk_out, scale), (dv_acc, dv_out, 1.0))):
            give_back(j, a).wait_recv()
            out[j, 0:rows, :] = (acc[j, halo:span, :] * factor).astype(jnp.bfloat16)
            out[j, rows:, :] = (
                acc[j, span:, :] * factor + halo_in[a, j].astype(jnp.float32)
            ).astype(jnp.bfloat16)

    def send_key_value(j):
        send_out(j, 1, dk_out, dk_hbm)
        send_out(j, 2, dv_out, dv_hbm)

    last = mine - 1

    def step(t, carry):
        @pl.when(t < mine)
        def _():
            wait_in(t, 0)
            for a, buf in enumerate((kb, vb)):
                forward(t, a, buf).start()

        @pl.when(t < last)
        def _():
            start_in(t + 1, 0)

        @pl.when(t == last)
        def _():
            def late(j, carry):
                send_out(j, 0, dq_out, dq_hbm)
                return carry

            lax.fori_loop(0, last - 1, late, 0)

        @pl.when((t >= 1) & (t <= mine))
        def _():
            j = t - 1

            @pl.when(j == 0)
            def _():
                wait_bytes(deltas.at[0 : GROUP - 1], del_recv.at[0])

            for a, buf in enumerate((kb, vb)):
                forward(j, a, buf).wait_recv()
            compute(j)
            halo_out[0, j] = (dk_acc[j, 0:halo, :] * scale).astype(jnp.bfloat16)
            halo_out[1, j] = dv_acc[j, 0:halo, :].astype(jnp.bfloat16)
            for a in range(2):
                give_back(j, a).start()

            @pl.when(t >= last)
            def _():
                send_out(j, 0, dq_out, dq_hbm)

        @pl.when(t < mine)
        def _():
            wait_in(t, 1)

        @pl.when(t < last)
        def _():
            start_in(t + 1, 1)

        @pl.when(t >= 2)
        def _():
            finish(t - 2)

        @pl.when(t == last)
        def _():
            def late(j, carry):
                send_key_value(j)
                return carry

            lax.fori_loop(0, last - 2, late, 0)

        @pl.when(t >= last)
        def _():
            send_key_value(t - 2)

        return carry

    lax.fori_loop(0, mine + 2, step, 0)

    wait_bytes(segs.at[0 : GROUP - 1], seg_send.at[0])
    wait_bytes(deltas.at[0 : GROUP - 1], del_send.at[0])

    def drain(j, carry):
        for a, buf in enumerate((kb, vb)):
            forward(j, a, buf).wait_send()
            give_back(j, a).wait_send()
        for a in range(3):
            wait_bytes(dq_out.at[j, 0 : (GROUP - 1) * rows], out_send.at[j, a])
            wait_bytes(dq_out.at[j], out_recv.at[j, a])
        return carry

    lax.fori_loop(0, mine, drain, 0)


def body(queries, keys, values, outputs, out_grad, segment_ids):
    rows, width = queries.shape
    mine = width // HEAD // GROUP
    halo, group = (WIN - 1) * rows, GROUP * rows
    bf16, f32, i32 = jnp.bfloat16, jnp.float32, jnp.int32
    dma = pltpu.SemaphoreType.DMA
    anywhere = pl.BlockSpec(memory_space=pltpu.HBM)
    return pl.pallas_call(
        kernel,
        out_shape=[jax.ShapeDtypeStruct((rows, width), bf16)] * 3,
        in_specs=[anywhere] * 6,
        out_specs=[anywhere] * 3,
        scratch_shapes=[
            pltpu.VMEM((mine, group, HEAD), bf16),
            pltpu.VMEM((mine, group, HEAD), bf16),
            pltpu.VMEM((mine, halo + group, HEAD), bf16),
            pltpu.VMEM((mine, halo + group, HEAD), bf16),
            pltpu.VMEM((rows, width), bf16),
            pltpu.VMEM((rows, width), bf16),
            pltpu.VMEM((1, rows), i32),
            pltpu.VMEM((8, rows), i32),
            pltpu.VMEM((WIN - 1 + GROUP, 8, rows), i32),
            pltpu.VMEM((GROUP, 8, rows), f32),
            pltpu.VMEM((GROUP, 8, rows), f32),
            pltpu.VMEM((GROUP, 8, rows), i32),
            pltpu.VMEM((mine, halo + group, HEAD), f32),
            pltpu.VMEM((mine, halo + group, HEAD), f32),
            pltpu.VMEM((mine, group, HEAD), bf16),
            pltpu.VMEM((mine, group, HEAD), bf16),
            pltpu.VMEM((mine, group, HEAD), bf16),
            pltpu.VMEM((2, mine, halo, HEAD), bf16),
            pltpu.VMEM((2, mine, halo, HEAD), bf16),
            dma((mine, 4)), dma((mine, 4)),
            dma((mine, 2)), dma((mine, 2)),
            dma((mine, 2)), dma((mine, 2)),
            dma((mine, 3)), dma((mine, 3)),
            dma((2,)), dma((2,)),
            dma((1,)), dma((1,)),
            dma((3,)),
        ],
        compiler_params=pltpu.CompilerParams(
            collective_id=0, has_side_effects=True, vmem_limit_bytes=50 * 1024 * 1024
        ),
        name="window_attention_grads",
    )(queries, keys, values, outputs, out_grad, segment_ids.reshape(1, rows))


def solution(mesh):
    part = P(("dp", "ctx"), None)
    return jax.shard_map(
        body,
        mesh=mesh,
        in_specs=(part, part, part, part, part, P(("dp", "ctx"))),
        out_specs=(part, part, part),
        check_vma=False,
    )
```

```python
import jax
import jax.numpy as jnp
from jax import lax
from jax.experimental import pallas as pl
from jax.experimental.pallas import tpu as pltpu
from jax.sharding import PartitionSpec as P

HEAD = 128
WIN = 4
WINDOW = 768
GROUP = 4
LOG2E = 1.4426950408889634
masked_score = -1e30
MESH = pl.DeviceIdType.MESH


def dot(a, b, dims):
    return lax.dot_general(a, b, (dims, ((), ())), preferred_element_type=jnp.float32)


def kernel(
    q_hbm, k_hbm, v_hbm, o_hbm, do_hbm, seg_hbm,
    dq_hbm, dk_hbm, dv_hbm,
    qb, dob, kb, vb, ob, dol, seg_row, segs, dsrc, deltas, lows,
    dk_acc, dv_acc, dq_out, dk_out, dv_out, halo_out, halo_in,
    in_send, in_recv, fwd_send, fwd_recv, ret_send, ret_recv, out_send, out_recv,
    seg_send, seg_recv, del_send, del_recv, loc_sem,
):
    rows = q_hbm.shape[0]
    heads = q_hbm.shape[1] // HEAD
    mine = heads // GROUP
    halo = (WIN - 1) * rows
    span = WIN * rows
    scale = HEAD ** (-0.5)
    twice = 2.0 * scale
    n_ctx = lax.axis_size("ctx")
    n_x = n_ctx // GROUP
    me = lax.axis_index("ctx")
    x = me // GROUP
    g = lax.rem(me, GROUP)
    y = g // 2
    c = lax.rem(g, 2)
    peers = [2 * (1 - y) + c, 2 * (1 - y) + (1 - c), 2 * y + (1 - c)]
    ahead = lax.rem(x + 1, n_x) * GROUP + g
    behind = lax.rem(x + n_x - 1, n_x) * GROUP + g

    o_copy = pltpu.make_async_copy(o_hbm, ob, loc_sem.at[0])
    do_copy = pltpu.make_async_copy(do_hbm, dol, loc_sem.at[1])
    seg_copy = pltpu.make_async_copy(seg_hbm, seg_row, loc_sem.at[2])
    seg_copy.start()
    o_copy.start()
    do_copy.start()

    barrier = pltpu.get_barrier_semaphore()
    for other in [x * GROUP + p for p in peers] + [ahead, behind]:
        pl.semaphore_signal(barrier, inc=1, device_id={"ctx": other}, device_id_type=MESH)
    pl.semaphore_wait(barrier, 5)

    def remote(src, dst, send, recv, to):
        return pltpu.make_async_remote_copy(
            src_ref=src, dst_ref=dst, send_sem=send, recv_sem=recv,
            device_id={"ctx": to}, device_id_type=MESH,
        )

    def wait_bytes(ref, sem):
        pltpu.make_async_copy(ref, ref, sem).wait()

    def columns(owner, j):
        return pl.ds(pl.multiple_of((owner * mine + j) * HEAD, HEAD), HEAD)

    def place(block, first):
        return pl.ds(pl.multiple_of(first + block * rows, rows), rows)

    arrays = [(k_hbm, kb, halo), (v_hbm, vb, halo), (q_hbm, qb, 0), (do_hbm, dob, 0)]

    seg_copy.wait()
    segs[WIN - 1 + g] = seg_row[...]
    for p in peers:
        remote(seg_row, segs.at[WIN - 1 + g], seg_send.at[0], seg_recv.at[0], x * GROUP + p).start()

    def start_in(j, stage):
        for a in range(2 * stage, 2 * stage + 2):
            src, dst, first = arrays[a]
            for p in peers:
                remote(
                    src.at[:, columns(p, j)], dst.at[j, place(g, first)],
                    in_send.at[j, a], in_recv.at[j, a], x * GROUP + p,
                ).start()
            pltpu.make_async_copy(
                src.at[:, columns(g, j)], dst.at[j, place(g, first)], in_recv.at[j, a]
            ).start()

    def wait_in(j, stage):
        for a in range(2 * stage, 2 * stage + 2):
            _, dst, first = arrays[a]
            wait_bytes(dst.at[j, first:], in_recv.at[j, a])
            wait_bytes(dst.at[j, 0 : (GROUP - 1) * rows], in_send.at[j, a])

    start_in(0, 0)
    start_in(0, 1)

    o_copy.wait()
    do_copy.wait()

    def one_delta(h, carry):
        cols = pl.ds(pl.multiple_of(h * HEAD, HEAD), HEAD)
        product = ob[:, cols].astype(jnp.float32) * dol[:, cols].astype(jnp.float32)
        dsrc[h // mine, pl.ds(lax.rem(h, mine), 1), :] = jnp.sum(product.T, axis=0, keepdims=True)
        return carry

    lax.fori_loop(0, heads, one_delta, 0)
    deltas[g] = dsrc[g]
    for p in peers:
        remote(dsrc.at[p], deltas.at[g], del_send.at[0], del_recv.at[0], x * GROUP + p).start()

    wait_bytes(segs.at[0 : GROUP - 1], seg_recv.at[0])
    seg_fwd = remote(segs.at[WIN:], segs.at[0 : WIN - 1], seg_send.at[1], seg_recv.at[1], ahead)
    seg_fwd.start()
    seg_fwd.wait_recv()
    seg_fwd.wait_send()
    for b in range(GROUP):
        ids = segs[WIN - 1 + b][0:1, :]
        low = lax.broadcasted_iota(jnp.int32, (1, rows), 1) + (span - rows - WINDOW + 1)
        first = jnp.zeros((1, rows), jnp.int32)
        for w in range(b, b + WIN):
            theirs = segs[w][0:1, :]
            if w < WIN - 1:
                theirs = jnp.where(x == 0, -1, theirs)
            for doc in range(8):
                fewer = jnp.sum((theirs < doc).astype(jnp.int32), axis=1, keepdims=True)
                first = first + jnp.where(ids == doc, fewer, 0)
        lows[b] = jnp.broadcast_to(jnp.maximum(low, first), (8, rows))

    def compute(j):
        dk_acc[j] = jnp.zeros(dk_acc.shape[1:], jnp.float32)
        dv_acc[j] = jnp.zeros(dv_acc.shape[1:], jnp.float32)

        def block(b, carry):
            window = pl.ds(pl.multiple_of(b * rows, rows), span)
            own = pl.ds(pl.multiple_of(b * rows, rows), rows)
            query, grad = qb[j, own, :], dob[j, own, :]
            key, value = kb[j, window, :], vb[j, window, :]
            place_k = lax.broadcasted_iota(jnp.int32, (span, rows), 0)
            place_q = lax.broadcasted_iota(jnp.int32, (span, rows), 1) + halo
            visible = (place_k <= place_q) & (place_k >= lows[b][0:1, :])
            scores = dot(key, query, ((1,), (1,))) * (scale * LOG2E)
            scores = jnp.where(visible, scores, masked_score)
            top = jnp.max(scores, axis=0, keepdims=True)
            weights = jnp.exp2(scores - top)
            total = jnp.sum(weights, axis=0, keepdims=True)
            probs = weights * (1.0 / total)
            probs_low = probs.astype(jnp.bfloat16)
            dv_acc[j, window, :] += dot(probs_low, grad, ((1,), (0,)))
            dprobs = dot(value, grad, ((1,), (1,)))
            delta = deltas[b, pl.ds(j, 1), :]
            dscores = (probs * (dprobs - delta)).astype(jnp.bfloat16)
            dk_acc[j, window, :] += dot(dscores, query, ((1,), (0,)))
            dq_out[j, own, :] = (dot(dscores, key, ((0,), (0,))) * twice).astype(jnp.bfloat16)
            return carry

        lax.fori_loop(0, GROUP, block, 0)

    def send_out(j, a, src, dst):
        for p in peers:
            remote(
                src.at[j, place(p, 0)], dst.at[:, columns(g, j)],
                out_send.at[j, a], out_recv.at[j, a], x * GROUP + p,
            ).start()
        pltpu.make_async_copy(
            src.at[j, place(g, 0)], dst.at[:, columns(g, j)], out_recv.at[j, a]
        ).start()

    def forward(j, a, buf):
        return remote(
            buf.at[j, span : span + halo], buf.at[j, 0:halo],
            fwd_send.at[j, a], fwd_recv.at[j, a], ahead,
        )

    def give_back(j, a):
        return remote(
            halo_out.at[a, j], halo_in.at[a, j], ret_send.at[j, a], ret_recv.at[j, a], behind
        )

    def finish(j):
        for a, (acc, out, factor) in enumerate(((dk_acc, dk_out, twice), (dv_acc, dv_out, 2.0))):
            give_back(j, a).wait_recv()
            out[j, 0:rows, :] = (acc[j, halo:span, :] * factor).astype(jnp.bfloat16)
            out[j, rows:, :] = (
                acc[j, span:, :] * factor + halo_in[a, j].astype(jnp.float32)
            ).astype(jnp.bfloat16)

    def send_key_value(j):
        send_out(j, 1, dk_out, dk_hbm)
        send_out(j, 2, dv_out, dv_hbm)

    last = mine - 1

    def step(t, carry):
        @pl.when(t < mine)
        def _():
            wait_in(t, 0)
            for a, buf in enumerate((kb, vb)):
                forward(t, a, buf).start()

        @pl.when(t < last)
        def _():
            start_in(t + 1, 0)

        @pl.when(t == last)
        def _():
            def late(j, carry):
                send_out(j, 0, dq_out, dq_hbm)
                return carry

            lax.fori_loop(0, last - 1, late, 0)

        @pl.when((t >= 1) & (t <= mine))
        def _():
            j = t - 1

            @pl.when(j == 0)
            def _():
                wait_bytes(deltas.at[0 : GROUP - 1], del_recv.at[0])

            for a, buf in enumerate((kb, vb)):
                forward(j, a, buf).wait_recv()
            compute(j)
            halo_out[0, j] = (dk_acc[j, 0:halo, :] * twice).astype(jnp.bfloat16)
            halo_out[1, j] = (dv_acc[j, 0:halo, :] * 2.0).astype(jnp.bfloat16)
            for a in range(2):
                give_back(j, a).start()

            @pl.when(t >= last)
            def _():
                send_out(j, 0, dq_out, dq_hbm)

        @pl.when(t < mine)
        def _():
            wait_in(t, 1)

        @pl.when(t < last)
        def _():
            start_in(t + 1, 1)

        @pl.when(t >= 2)
        def _():
            finish(t - 2)

        @pl.when(t == last)
        def _():
            def late(j, carry):
                send_key_value(j)
                return carry

            lax.fori_loop(0, last - 2, late, 0)

        @pl.when(t >= last)
        def _():
            send_key_value(t - 2)

        return carry

    lax.fori_loop(0, mine + 2, step, 0)

    wait_bytes(segs.at[0 : GROUP - 1], seg_send.at[0])
    wait_bytes(deltas.at[0 : GROUP - 1], del_send.at[0])

    def drain(j, carry):
        for a, buf in enumerate((kb, vb)):
            forward(j, a, buf).wait_send()
            give_back(j, a).wait_send()
        for a in range(3):
            wait_bytes(dq_out.at[j, 0 : (GROUP - 1) * rows], out_send.at[j, a])
            wait_bytes(dq_out.at[j], out_recv.at[j, a])
        return carry

    lax.fori_loop(0, mine, drain, 0)


def body(queries, keys, values, outputs, out_grad, segment_ids):
    rows, width = queries.shape
    mine = width // HEAD // GROUP
    halo, group = (WIN - 1) * rows, GROUP * rows
    bf16, f32, i32 = jnp.bfloat16, jnp.float32, jnp.int32
    dma = pltpu.SemaphoreType.DMA
    anywhere = pl.BlockSpec(memory_space=pltpu.HBM)
    doubled = pl.pallas_call(
        kernel,
        out_shape=[jax.ShapeDtypeStruct((rows, width), bf16)] * 3,
        in_specs=[anywhere] * 6,
        out_specs=[anywhere] * 3,
        scratch_shapes=[
            pltpu.VMEM((mine, group, HEAD), bf16),
            pltpu.VMEM((mine, group, HEAD), bf16),
            pltpu.VMEM((mine, halo + group, HEAD), bf16),
            pltpu.VMEM((mine, halo + group, HEAD), bf16),
            pltpu.VMEM((rows, width), bf16),
            pltpu.VMEM((rows, width), bf16),
            pltpu.VMEM((1, rows), i32),
            pltpu.VMEM((WIN - 1 + GROUP, 1, rows), i32),
            pltpu.VMEM((GROUP, mine, rows), f32),
            pltpu.VMEM((GROUP, mine, rows), f32),
            pltpu.VMEM((GROUP, 8, rows), i32),
            pltpu.VMEM((mine, halo + group, HEAD), f32),
            pltpu.VMEM((mine, halo + group, HEAD), f32),
            pltpu.VMEM((mine, group, HEAD), bf16),
            pltpu.VMEM((mine, group, HEAD), bf16),
            pltpu.VMEM((mine, group, HEAD), bf16),
            pltpu.VMEM((2, mine, halo, HEAD), bf16),
            pltpu.VMEM((2, mine, halo, HEAD), bf16),
            dma((mine, 4)), dma((mine, 4)),
            dma((mine, 2)), dma((mine, 2)),
            dma((mine, 2)), dma((mine, 2)),
            dma((mine, 3)), dma((mine, 3)),
            dma((2,)), dma((2,)),
            dma((1,)), dma((1,)),
            dma((3,)),
        ],
        compiler_params=pltpu.CompilerParams(
            collective_id=0, has_side_effects=True, vmem_limit_bytes=50 * 1024 * 1024
        ),
        name="window_attention_grads",
    )(queries, keys, values, outputs, out_grad, segment_ids.reshape(1, rows))
    return tuple(grad * 0.5 for grad in doubled)


def solution(mesh):
    part = P(("dp", "ctx"), None)
    return jax.shard_map(
        body,
        mesh=mesh,
        in_specs=(part, part, part, part, part, P(("dp", "ctx"))),
        out_specs=(part, part, part),
        check_vma=False,
    )
```

```python
import jax
import jax.numpy as jnp
from jax import lax
from jax.experimental import pallas as pl
from jax.experimental.pallas import tpu as pltpu
from jax.sharding import PartitionSpec as P

HEAD = 128
WIN = 4
WINDOW = 768
GROUP = 4
DEPTH = 3
LOG2E = 1.4426950408889634
masked_score = -1e30
MESH = pl.DeviceIdType.MESH


def dot(a, b, dims):
    return lax.dot_general(a, b, (dims, ((), ())), preferred_element_type=jnp.float32)


def kernel(
    q_hbm, k_hbm, v_hbm, o_hbm, do_hbm, seg_hbm,
    dq_hbm, dk_hbm, dv_hbm,
    qb, dob, kb, vb, ob, dol, seg_row, segs, dsrc, deltas, lows,
    dk_acc, dv_acc, dq_out, dk_out, dv_out, halo_out, halo_in,
    in_send, in_recv, fwd_send, fwd_recv, ret_send, ret_recv, out_send, out_recv,
    seg_send, seg_recv, del_send, del_recv, loc_sem,
):
    rows = q_hbm.shape[0]
    heads = q_hbm.shape[1] // HEAD
    mine = heads // GROUP
    halo = (WIN - 1) * rows
    span = WIN * rows
    scale = HEAD ** (-0.5)
    twice = 2.0 * scale
    n_ctx = lax.axis_size("ctx")
    n_x = n_ctx // GROUP
    me = lax.axis_index("ctx")
    x = me // GROUP
    g = lax.rem(me, GROUP)
    y = g // 2
    c = lax.rem(g, 2)
    peers = [2 * (1 - y) + c, 2 * (1 - y) + (1 - c), 2 * y + (1 - c)]
    ahead = lax.rem(x + 1, n_x) * GROUP + g
    behind = lax.rem(x + n_x - 1, n_x) * GROUP + g

    o_copy = pltpu.make_async_copy(o_hbm, ob, loc_sem.at[0])
    do_copy = pltpu.make_async_copy(do_hbm, dol, loc_sem.at[1])
    seg_copy = pltpu.make_async_copy(seg_hbm, seg_row, loc_sem.at[2])
    seg_copy.start()
    o_copy.start()
    do_copy.start()

    barrier = pltpu.get_barrier_semaphore()
    for other in [x * GROUP + p for p in peers] + [ahead, behind]:
        pl.semaphore_signal(barrier, inc=1, device_id={"ctx": other}, device_id_type=MESH)
    pl.semaphore_wait(barrier, 5)

    def remote(src, dst, send, recv, to):
        return pltpu.make_async_remote_copy(
            src_ref=src, dst_ref=dst, send_sem=send, recv_sem=recv,
            device_id={"ctx": to}, device_id_type=MESH,
        )

    def wait_bytes(ref, sem):
        pltpu.make_async_copy(ref, ref, sem).wait()

    def columns(owner, j):
        return pl.ds(pl.multiple_of((owner * mine + j) * HEAD, HEAD), HEAD)

    def place(block, first):
        return pl.ds(pl.multiple_of(first + block * rows, rows), rows)

    arrays = [(k_hbm, kb, halo), (v_hbm, vb, halo), (q_hbm, qb, 0), (do_hbm, dob, 0)]

    def start_in(j, stage):
        for a in range(2 * stage, 2 * stage + 2):
            src, dst, first = arrays[a]
            for p in peers:
                remote(
                    src.at[:, columns(p, j)], dst.at[j, place(g, first)],
                    in_send.at[j, a], in_recv.at[j, a], x * GROUP + p,
                ).start()
            pltpu.make_async_copy(
                src.at[:, columns(g, j)], dst.at[j, place(g, first)], in_recv.at[j, a]
            ).start()

    def start_ahead(j, stage):
        later, kind = j + (stage + DEPTH) // 2, (stage + DEPTH) % 2

        @pl.when(later < mine)
        def _():
            start_in(later, kind)

    def wait_in(j, stage):
        for a in range(2 * stage, 2 * stage + 2):
            _, dst, first = arrays[a]
            wait_bytes(dst.at[j, first:], in_recv.at[j, a])
            wait_bytes(dst.at[j, 0 : (GROUP - 1) * rows], in_send.at[j, a])

    start_in(0, 0)

    seg_copy.wait()
    segs[WIN - 1 + g] = seg_row[...]
    for p in peers:
        remote(seg_row, segs.at[WIN - 1 + g], seg_send.at[0], seg_recv.at[0], x * GROUP + p).start()

    for stage in range(1, DEPTH):
        start_in(stage // 2, stage % 2)

    o_copy.wait()
    do_copy.wait()

    def one_delta(h, carry):
        cols = pl.ds(pl.multiple_of(h * HEAD, HEAD), HEAD)
        product = ob[:, cols].astype(jnp.float32) * dol[:, cols].astype(jnp.float32)
        dsrc[h // mine, pl.ds(lax.rem(h, mine), 1), :] = jnp.sum(product.T, axis=0, keepdims=True)
        return carry

    lax.fori_loop(0, heads, one_delta, 0)
    deltas[g] = dsrc[g]
    for p in peers:
        remote(dsrc.at[p], deltas.at[g], del_send.at[0], del_recv.at[0], x * GROUP + p).start()

    wait_bytes(segs.at[0 : GROUP - 1], seg_recv.at[0])
    seg_fwd = remote(segs.at[WIN:], segs.at[0 : WIN - 1], seg_send.at[1], seg_recv.at[1], ahead)
    seg_fwd.start()
    seg_fwd.wait_recv()
    seg_fwd.wait_send()
    for b in range(GROUP):
        ids = segs[WIN - 1 + b][0:1, :]
        low = lax.broadcasted_iota(jnp.int32, (1, rows), 1) + (span - rows - WINDOW + 1)
        first = jnp.zeros((1, rows), jnp.int32)
        for w in range(b, b + WIN):
            theirs = segs[w][0:1, :]
            if w < WIN - 1:
                theirs = jnp.where(x == 0, -1, theirs)
            for doc in range(8):
                fewer = jnp.sum((theirs < doc).astype(jnp.int32), axis=1, keepdims=True)
                first = first + jnp.where(ids == doc, fewer, 0)
        lows[b] = jnp.broadcast_to(jnp.maximum(low, first), (8, rows))

    def compute(j):
        dk_acc[j] = jnp.zeros(dk_acc.shape[1:], jnp.float32)
        dv_acc[j] = jnp.zeros(dv_acc.shape[1:], jnp.float32)

        def block(b, carry):
            window = pl.ds(pl.multiple_of(b * rows, rows), span)
            own = pl.ds(pl.multiple_of(b * rows, rows), rows)
            query, grad = qb[j, own, :], dob[j, own, :]
            key, value = kb[j, window, :], vb[j, window, :]
            place_k = lax.broadcasted_iota(jnp.int32, (span, rows), 0)
            place_q = lax.broadcasted_iota(jnp.int32, (span, rows), 1) + halo
            visible = (place_k <= place_q) & (place_k >= lows[b][0:1, :])
            scores = dot(key, query, ((1,), (1,))) * (scale * LOG2E)
            scores = jnp.where(visible, scores, masked_score)
            top = jnp.max(scores, axis=0, keepdims=True)
            weights = jnp.exp2(scores - top)
            total = jnp.sum(weights, axis=0, keepdims=True)
            probs = weights * (1.0 / total)
            probs_low = probs.astype(jnp.bfloat16)
            dv_acc[j, window, :] += dot(probs_low, grad, ((1,), (0,)))
            dprobs = dot(value, grad, ((1,), (1,)))
            delta = deltas[b, pl.ds(j, 1), :]
            dscores = (probs * (dprobs - delta)).astype(jnp.bfloat16)
            dk_acc[j, window, :] += dot(dscores, query, ((1,), (0,)))
            dq_out[j, own, :] = (dot(dscores, key, ((0,), (0,))) * twice).astype(jnp.bfloat16)
            return carry

        lax.fori_loop(0, GROUP, block, 0)

    def send_out(j, a, src, dst):
        for p in peers:
            remote(
                src.at[j, place(p, 0)], dst.at[:, columns(g, j)],
                out_send.at[j, a], out_recv.at[j, a], x * GROUP + p,
            ).start()
        pltpu.make_async_copy(
            src.at[j, place(g, 0)], dst.at[:, columns(g, j)], out_recv.at[j, a]
        ).start()

    def forward(j, a, buf):
        return remote(
            buf.at[j, span : span + halo], buf.at[j, 0:halo],
            fwd_send.at[j, a], fwd_recv.at[j, a], ahead,
        )

    def give_back(j, a):
        return remote(
            halo_out.at[a, j], halo_in.at[a, j], ret_send.at[j, a], ret_recv.at[j, a], behind
        )

    def finish(j):
        for a, (acc, out, factor) in enumerate(((dk_acc, dk_out, twice), (dv_acc, dv_out, 2.0))):
            give_back(j, a).wait_recv()
            out[j, 0:rows, :] = (acc[j, halo:span, :] * factor).astype(jnp.bfloat16)
            out[j, rows:, :] = (
                acc[j, span:, :] * factor + halo_in[a, j].astype(jnp.float32)
            ).astype(jnp.bfloat16)

    def send_key_value(j):
        send_out(j, 1, dk_out, dk_hbm)
        send_out(j, 2, dv_out, dv_hbm)

    last = mine - 1

    def step(t, carry):
        @pl.when(t < mine)
        def _():
            wait_in(t, 0)
            for a, buf in enumerate((kb, vb)):
                forward(t, a, buf).start()

        start_ahead(t, 0)

        @pl.when(t == last)
        def _():
            def late(j, carry):
                send_out(j, 0, dq_out, dq_hbm)
                return carry

            lax.fori_loop(0, last - 1, late, 0)

        @pl.when((t >= 1) & (t <= mine))
        def _():
            j = t - 1

            @pl.when(j == 0)
            def _():
                wait_bytes(deltas.at[0 : GROUP - 1], del_recv.at[0])

            for a, buf in enumerate((kb, vb)):
                forward(j, a, buf).wait_recv()
            compute(j)
            halo_out[0, j] = (dk_acc[j, 0:halo, :] * twice).astype(jnp.bfloat16)
            halo_out[1, j] = (dv_acc[j, 0:halo, :] * 2.0).astype(jnp.bfloat16)
            for a in range(2):
                give_back(j, a).start()

            @pl.when(t >= last)
            def _():
                send_out(j, 0, dq_out, dq_hbm)

        @pl.when(t < mine)
        def _():
            wait_in(t, 1)

        start_ahead(t, 1)

        @pl.when(t >= 2)
        def _():
            finish(t - 2)

        @pl.when(t == last)
        def _():
            def late(j, carry):
                send_key_value(j)
                return carry

            lax.fori_loop(0, last - 2, late, 0)

        @pl.when(t >= last)
        def _():
            send_key_value(t - 2)

        return carry

    lax.fori_loop(0, mine + 2, step, 0)

    wait_bytes(segs.at[0 : GROUP - 1], seg_send.at[0])
    wait_bytes(deltas.at[0 : GROUP - 1], del_send.at[0])

    def drain(j, carry):
        for a, buf in enumerate((kb, vb)):
            forward(j, a, buf).wait_send()
            give_back(j, a).wait_send()
        for a in range(3):
            wait_bytes(dq_out.at[j, 0 : (GROUP - 1) * rows], out_send.at[j, a])
            wait_bytes(dq_out.at[j], out_recv.at[j, a])
        return carry

    lax.fori_loop(0, mine, drain, 0)


def body(queries, keys, values, outputs, out_grad, segment_ids):
    rows, width = queries.shape
    mine = width // HEAD // GROUP
    halo, group = (WIN - 1) * rows, GROUP * rows
    bf16, f32, i32 = jnp.bfloat16, jnp.float32, jnp.int32
    dma = pltpu.SemaphoreType.DMA
    anywhere = pl.BlockSpec(memory_space=pltpu.HBM)
    doubled = pl.pallas_call(
        kernel,
        out_shape=[jax.ShapeDtypeStruct((rows, width), bf16)] * 3,
        in_specs=[anywhere] * 6,
        out_specs=[anywhere] * 3,
        scratch_shapes=[
            pltpu.VMEM((mine, group, HEAD), bf16),
            pltpu.VMEM((mine, group, HEAD), bf16),
            pltpu.VMEM((mine, halo + group, HEAD), bf16),
            pltpu.VMEM((mine, halo + group, HEAD), bf16),
            pltpu.VMEM((rows, width), bf16),
            pltpu.VMEM((rows, width), bf16),
            pltpu.VMEM((1, rows), i32),
            pltpu.VMEM((WIN - 1 + GROUP, 1, rows), i32),
            pltpu.VMEM((GROUP, mine, rows), f32),
            pltpu.VMEM((GROUP, mine, rows), f32),
            pltpu.VMEM((GROUP, 8, rows), i32),
            pltpu.VMEM((mine, halo + group, HEAD), f32),
            pltpu.VMEM((mine, halo + group, HEAD), f32),
            pltpu.VMEM((mine, group, HEAD), bf16),
            pltpu.VMEM((mine, group, HEAD), bf16),
            pltpu.VMEM((mine, group, HEAD), bf16),
            pltpu.VMEM((2, mine, halo, HEAD), bf16),
            pltpu.VMEM((2, mine, halo, HEAD), bf16),
            dma((mine, 4)), dma((mine, 4)),
            dma((mine, 2)), dma((mine, 2)),
            dma((mine, 2)), dma((mine, 2)),
            dma((mine, 3)), dma((mine, 3)),
            dma((2,)), dma((2,)),
            dma((1,)), dma((1,)),
            dma((3,)),
        ],
        compiler_params=pltpu.CompilerParams(
            collective_id=0, has_side_effects=True, vmem_limit_bytes=50 * 1024 * 1024
        ),
        name="window_attention_grads",
    )(queries, keys, values, outputs, out_grad, segment_ids.reshape(1, rows))
    return tuple(grad * 0.5 for grad in doubled)


def solution(mesh):
    part = P(("dp", "ctx"), None)
    return jax.shard_map(
        body,
        mesh=mesh,
        in_specs=(part, part, part, part, part, P(("dp", "ctx"))),
        out_specs=(part, part, part),
        check_vma=False,
    )
```

```python
import jax
import jax.numpy as jnp
from jax import lax
from jax.experimental import pallas as pl
from jax.experimental.pallas import tpu as pltpu
from jax.sharding import PartitionSpec as P

HEAD = 128
WIN = 4
WINDOW = 768
GROUP = 4
LOG2E = 1.4426950408889634
masked_score = -1e30
MESH = pl.DeviceIdType.MESH


def dot(a, b, dims):
    return lax.dot_general(a, b, (dims, ((), ())), preferred_element_type=jnp.float32)


def kernel(
    q_hbm, k_hbm, v_hbm, o_hbm, do_hbm, seg_hbm,
    dq_hbm, dk_hbm, dv_hbm,
    qb, dob, kb, vb, ob, dol, seg_row, segs, dsrc, deltas, lows,
    dk_acc, dv_acc, dq_out, dk_out, dv_out, halo_out, halo_in,
    in_send, in_recv, fwd_send, fwd_recv, ret_send, ret_recv, out_send, out_recv,
    seg_send, seg_recv, del_send, del_recv, loc_sem,
):
    rows = q_hbm.shape[0]
    heads = q_hbm.shape[1] // HEAD
    mine = heads // GROUP
    halo = (WIN - 1) * rows
    span = WIN * rows
    scale = HEAD ** (-0.5)
    twice = 2.0 * scale
    n_ctx = lax.axis_size("ctx")
    n_x = n_ctx // GROUP
    me = lax.axis_index("ctx")
    x = me // GROUP
    g = lax.rem(me, GROUP)
    y = g // 2
    c = lax.rem(g, 2)
    peers = [2 * (1 - y) + c, 2 * (1 - y) + (1 - c), 2 * y + (1 - c)]
    ahead = lax.rem(x + 1, n_x) * GROUP + g
    behind = lax.rem(x + n_x - 1, n_x) * GROUP + g

    o_copy = pltpu.make_async_copy(o_hbm, ob, loc_sem.at[0])
    do_copy = pltpu.make_async_copy(do_hbm, dol, loc_sem.at[1])
    seg_copy = pltpu.make_async_copy(seg_hbm, seg_row, loc_sem.at[2])
    seg_copy.start()

    barrier = pltpu.get_barrier_semaphore()
    for other in [x * GROUP + p for p in peers] + [ahead, behind]:
        pl.semaphore_signal(barrier, inc=1, device_id={"ctx": other}, device_id_type=MESH)
    pl.semaphore_wait(barrier, 5)

    def remote(src, dst, send, recv, to):
        return pltpu.make_async_remote_copy(
            src_ref=src, dst_ref=dst, send_sem=send, recv_sem=recv,
            device_id={"ctx": to}, device_id_type=MESH,
        )

    def wait_bytes(ref, sem):
        pltpu.make_async_copy(ref, ref, sem).wait()

    def columns(owner, j):
        return pl.ds(pl.multiple_of((owner * mine + j) * HEAD, HEAD), HEAD)

    def place(block, first):
        return pl.ds(pl.multiple_of(first + block * rows, rows), rows)

    arrays = [(k_hbm, kb, halo), (v_hbm, vb, halo), (q_hbm, qb, 0), (do_hbm, dob, 0)]

    seg_copy.wait()
    segs[WIN - 1 + g] = seg_row[...]
    for p in peers:
        remote(seg_row, segs.at[WIN - 1 + g], seg_send.at[0], seg_recv.at[0], x * GROUP + p).start()

    def start_in(j, stage):
        for a in range(2 * stage, 2 * stage + 2):
            src, dst, first = arrays[a]
            for p in peers:
                remote(
                    src.at[:, columns(p, j)], dst.at[j, place(g, first)],
                    in_send.at[j, a], in_recv.at[j, a], x * GROUP + p,
                ).start()
            pltpu.make_async_copy(
                src.at[:, columns(g, j)], dst.at[j, place(g, first)], in_recv.at[j, a]
            ).start()

    def wait_in(j, stage):
        for a in range(2 * stage, 2 * stage + 2):
            _, dst, first = arrays[a]
            wait_bytes(dst.at[j, first:], in_recv.at[j, a])
            wait_bytes(dst.at[j, 0 : (GROUP - 1) * rows], in_send.at[j, a])

    start_in(0, 0)
    start_in(0, 1)

    o_copy.start()
    do_copy.start()

    o_copy.wait()
    do_copy.wait()

    def one_delta(h, carry):
        cols = pl.ds(pl.multiple_of(h * HEAD, HEAD), HEAD)
        product = ob[:, cols].astype(jnp.float32) * dol[:, cols].astype(jnp.float32)
        dsrc[h // mine, pl.ds(lax.rem(h, mine), 1), :] = jnp.sum(product.T, axis=0, keepdims=True)
        return carry

    lax.fori_loop(0, heads, one_delta, 0)
    deltas[g] = dsrc[g]
    for p in peers:
        remote(dsrc.at[p], deltas.at[g], del_send.at[0], del_recv.at[0], x * GROUP + p).start()

    wait_bytes(segs.at[0 : GROUP - 1], seg_recv.at[0])
    seg_fwd = remote(segs.at[WIN:], segs.at[0 : WIN - 1], seg_send.at[1], seg_recv.at[1], ahead)
    seg_fwd.start()
    seg_fwd.wait_recv()
    seg_fwd.wait_send()
    for b in range(GROUP):
        ids = segs[WIN - 1 + b][0:1, :]
        low = lax.broadcasted_iota(jnp.int32, (1, rows), 1) + (span - rows - WINDOW + 1)
        first = jnp.zeros((1, rows), jnp.int32)
        for w in range(b, b + WIN):
            theirs = segs[w][0:1, :]
            if w < WIN - 1:
                theirs = jnp.where(x == 0, -1, theirs)
            for doc in range(8):
                fewer = jnp.sum((theirs < doc).astype(jnp.int32), axis=1, keepdims=True)
                first = first + jnp.where(ids == doc, fewer, 0)
        lows[b] = jnp.broadcast_to(jnp.maximum(low, first), (8, rows))

    def compute(j):
        dk_acc[j] = jnp.zeros(dk_acc.shape[1:], jnp.float32)
        dv_acc[j] = jnp.zeros(dv_acc.shape[1:], jnp.float32)

        def block(b, carry):
            window = pl.ds(pl.multiple_of(b * rows, rows), span)
            own = pl.ds(pl.multiple_of(b * rows, rows), rows)
            query, grad = qb[j, own, :], dob[j, own, :]
            key, value = kb[j, window, :], vb[j, window, :]
            place_k = lax.broadcasted_iota(jnp.int32, (span, rows), 0)
            place_q = lax.broadcasted_iota(jnp.int32, (span, rows), 1) + halo
            visible = (place_k <= place_q) & (place_k >= lows[b][0:1, :])
            scores = dot(key, query, ((1,), (1,))) * (scale * LOG2E)
            scores = jnp.where(visible, scores, masked_score)
            top = jnp.max(scores, axis=0, keepdims=True)
            weights = jnp.exp2(scores - top)
            total = jnp.sum(weights, axis=0, keepdims=True)
            probs = weights * (1.0 / total)
            probs_low = probs.astype(jnp.bfloat16)
            dv_acc[j, window, :] += dot(probs_low, grad, ((1,), (0,)))
            dprobs = dot(value, grad, ((1,), (1,)))
            delta = deltas[b, pl.ds(j, 1), :]
            dscores = (probs * (dprobs - delta)).astype(jnp.bfloat16)
            dk_acc[j, window, :] += dot(dscores, query, ((1,), (0,)))
            dq_out[j, own, :] = (dot(dscores, key, ((0,), (0,))) * twice).astype(jnp.bfloat16)
            return carry

        lax.fori_loop(0, GROUP, block, 0)

    def send_out(j, a, src, dst):
        for p in peers:
            remote(
                src.at[j, place(p, 0)], dst.at[:, columns(g, j)],
                out_send.at[j, a], out_recv.at[j, a], x * GROUP + p,
            ).start()
        pltpu.make_async_copy(
            src.at[j, place(g, 0)], dst.at[:, columns(g, j)], out_recv.at[j, a]
        ).start()

    def forward(j, a, buf):
        return remote(
            buf.at[j, span : span + halo], buf.at[j, 0:halo],
            fwd_send.at[j, a], fwd_recv.at[j, a], ahead,
        )

    def give_back(j, a):
        return remote(
            halo_out.at[a, j], halo_in.at[a, j], ret_send.at[j, a], ret_recv.at[j, a], behind
        )

    def finish(j):
        for a, (acc, out, factor) in enumerate(((dk_acc, dk_out, twice), (dv_acc, dv_out, 2.0))):
            give_back(j, a).wait_recv()
            out[j, 0:rows, :] = (acc[j, halo:span, :] * factor).astype(jnp.bfloat16)
            out[j, rows:, :] = (
                acc[j, span:, :] * factor + halo_in[a, j].astype(jnp.float32)
            ).astype(jnp.bfloat16)

    def send_key_value(j):
        send_out(j, 1, dk_out, dk_hbm)
        send_out(j, 2, dv_out, dv_hbm)

    last = mine - 1

    def step(t, carry):
        @pl.when(t < mine)
        def _():
            wait_in(t, 0)
            for a, buf in enumerate((kb, vb)):
                forward(t, a, buf).start()

        @pl.when(t < last)
        def _():
            start_in(t + 1, 0)

        @pl.when(t == last)
        def _():
            def late(j, carry):
                send_out(j, 0, dq_out, dq_hbm)
                return carry

            lax.fori_loop(0, last - 1, late, 0)

        @pl.when((t >= 1) & (t <= mine))
        def _():
            j = t - 1

            @pl.when(j == 0)
            def _():
                wait_bytes(deltas.at[0 : GROUP - 1], del_recv.at[0])

            for a, buf in enumerate((kb, vb)):
                forward(j, a, buf).wait_recv()
            compute(j)
            halo_out[0, j] = (dk_acc[j, 0:halo, :] * twice).astype(jnp.bfloat16)
            halo_out[1, j] = (dv_acc[j, 0:halo, :] * 2.0).astype(jnp.bfloat16)
            for a in range(2):
                give_back(j, a).start()

            @pl.when(t >= last)
            def _():
                send_out(j, 0, dq_out, dq_hbm)

        @pl.when(t < mine)
        def _():
            wait_in(t, 1)

        @pl.when(t < last)
        def _():
            start_in(t + 1, 1)

        @pl.when(t >= 2)
        def _():
            finish(t - 2)

        @pl.when(t == last)
        def _():
            def late(j, carry):
                send_key_value(j)
                return carry

            lax.fori_loop(0, last - 2, late, 0)

        @pl.when(t >= last)
        def _():
            send_key_value(t - 2)

        return carry

    lax.fori_loop(0, mine + 2, step, 0)

    wait_bytes(segs.at[0 : GROUP - 1], seg_send.at[0])
    wait_bytes(deltas.at[0 : GROUP - 1], del_send.at[0])

    def drain(j, carry):
        for a, buf in enumerate((kb, vb)):
            forward(j, a, buf).wait_send()
            give_back(j, a).wait_send()
        for a in range(3):
            wait_bytes(dq_out.at[j, 0 : (GROUP - 1) * rows], out_send.at[j, a])
            wait_bytes(dq_out.at[j], out_recv.at[j, a])
        return carry

    lax.fori_loop(0, mine, drain, 0)


def body(queries, keys, values, outputs, out_grad, segment_ids):
    rows, width = queries.shape
    mine = width // HEAD // GROUP
    halo, group = (WIN - 1) * rows, GROUP * rows
    bf16, f32, i32 = jnp.bfloat16, jnp.float32, jnp.int32
    dma = pltpu.SemaphoreType.DMA
    anywhere = pl.BlockSpec(memory_space=pltpu.HBM)
    doubled = pl.pallas_call(
        kernel,
        out_shape=[jax.ShapeDtypeStruct((rows, width), bf16)] * 3,
        in_specs=[anywhere] * 6,
        out_specs=[anywhere] * 3,
        scratch_shapes=[
            pltpu.VMEM((mine, group, HEAD), bf16),
            pltpu.VMEM((mine, group, HEAD), bf16),
            pltpu.VMEM((mine, halo + group, HEAD), bf16),
            pltpu.VMEM((mine, halo + group, HEAD), bf16),
            pltpu.VMEM((rows, width), bf16),
            pltpu.VMEM((rows, width), bf16),
            pltpu.VMEM((1, rows), i32),
            pltpu.VMEM((WIN - 1 + GROUP, 1, rows), i32),
            pltpu.VMEM((GROUP, mine, rows), f32),
            pltpu.VMEM((GROUP, mine, rows), f32),
            pltpu.VMEM((GROUP, 8, rows), i32),
            pltpu.VMEM((mine, halo + group, HEAD), f32),
            pltpu.VMEM((mine, halo + group, HEAD), f32),
            pltpu.VMEM((mine, group, HEAD), bf16),
            pltpu.VMEM((mine, group, HEAD), bf16),
            pltpu.VMEM((mine, group, HEAD), bf16),
            pltpu.VMEM((2, mine, halo, HEAD), bf16),
            pltpu.VMEM((2, mine, halo, HEAD), bf16),
            dma((mine, 4)), dma((mine, 4)),
            dma((mine, 2)), dma((mine, 2)),
            dma((mine, 2)), dma((mine, 2)),
            dma((mine, 3)), dma((mine, 3)),
            dma((2,)), dma((2,)),
            dma((1,)), dma((1,)),
            dma((3,)),
        ],
        compiler_params=pltpu.CompilerParams(
            collective_id=0, has_side_effects=True, vmem_limit_bytes=50 * 1024 * 1024
        ),
        name="window_attention_grads",
    )(queries, keys, values, outputs, out_grad, segment_ids.reshape(1, rows))
    return tuple(grad * 0.5 for grad in doubled)


def solution(mesh):
    part = P(("dp", "ctx"), None)
    return jax.shard_map(
        body,
        mesh=mesh,
        in_specs=(part, part, part, part, part, P(("dp", "ctx"))),
        out_specs=(part, part, part),
        check_vma=False,
    )
```
